256 devices in a mesh: band: 32 (over y, z_hi, core), grid: 8 (over z_lo, x).
Axes of the slice: x: 4, y: 4, z: 8 (z_hi: 4, z_lo: 2; z = z_hi * 2 + z_lo), core: 2. Of those that a mesh axis runs over, the one named last changes fastest.
Arguments:
- orbitals: float32 [128, 64, 80, 128], P('band', 'grid'), as said below
- potential: float32 [64, 80, 128], P('grid'), may hold values from -2 to 1
- projectors: float32 [4, 16384], P(None, 'grid'), may hold values from -3 to 3
- coupling: float32 [64, 4, 4], P('grid'), may hold values from -4 to 4
- entry_cell: int32 [16384], P('grid'), may hold values from 0 to 81919
- entry_atom: int32 [16384], P('grid'), may hold values from -1 to 63, as said below
Outputs:
- block_out: float32 [128, 64, 80, 128], P('band', 'grid')
The draws below stay inside these ranges and needn't reach their ends.
Inputs may be any that keep to these rules, and one draw needn't show every extreme that they name: `entry_atom`: atoms a*8 to (a+1)*8 - 1 belong to domain a. A live slot of domain g names an atom of domain g-1, g or g+1; a domain's live slots come first; one domain has all 2048 slots live and another only 512 in every draw, the others 2048/4, 1024, 1536 or 2048. Each orbital is its own rough field plus a multiple of one field common to all orbitals, scaled per orbital.
All inputs are finite; a program needn't handle non-finite values.
Results may differ from the reference program's by a relative error of at most 0.00019.
Values sent between devices are 32-bit elements; how exact they have to be, the bound alone decides.
A program may use at most 128 MiB of HBM per device.

```python
import math
import jax
import jax.numpy as jnp
from jax import lax

ORB_DEV = 4
NORB = 128
CX = 8
NY = 80
NZ = 128
NX = 64
NPROJ = 4
ATOM_DEV = 8
NATOM = 64
ENT = 2048
N_BAND = 32
N_GRID = 8


def draw_orbitals(key, part):
    key = jax.random.fold_in(key, 11)
    key_own, key_common, key_mix, key_scale = jax.random.split(key, 4)
    shape_all = (NORB, NX, NY, NZ)
    own_part = jax.random.normal(key_own, shape_all, jnp.float32)
    common = jax.random.normal(key_common, (NX, NY, NZ), jnp.float32)
    mixing = 0.7 * jax.random.normal(key_mix, (NORB, 1, 1, 1), jnp.float32)
    scales = jnp.exp(jax.random.uniform(key_scale, (NORB, 1, 1, 1), jnp.float32, math.log(0.3), math.log(3.0)))
    return scales * (own_part + mixing * common[None])


def draw_entry_atom(key, part):
    key = jax.random.fold_in(key, 23)
    key_level, key_full, key_offset, key_atom = jax.random.split(key, 4)
    domain_index = jnp.arange(N_GRID, dtype=jnp.int32)
    fill_level = jax.random.randint(key_level, (N_GRID,), 0, 4)
    full_domain = jax.random.randint(key_full, (), 0, N_GRID)
    fill_level = jnp.where(domain_index == full_domain, 3, fill_level)
    fill_level = jnp.where(domain_index == (full_domain + 1) % N_GRID, 0, fill_level)
    live_count = ENT * (fill_level + 1) // 4
    slot_index = jnp.arange(ENT, dtype=jnp.int32)
    offset = jax.random.randint(key_offset, (N_GRID, ENT), -1, 2)
    owner_domain = jnp.clip(domain_index[:, None] + offset, 0, N_GRID - 1)
    atom_index = owner_domain * ATOM_DEV + jax.random.randint(key_atom, (N_GRID, ENT), 0, ATOM_DEV)
    atom_index = atom_index.at[N_GRID - 1, 0].set(N_GRID * ATOM_DEV - 1)
    atom_index = jnp.where(slot_index[None, :] < live_count[:, None], atom_index, -1)
    return atom_index.reshape(-1).astype(jnp.int32)


def place_ends(drawn, key, low, top_value):
    place = [jax.random.randint(jax.random.fold_in(key, axis), (), 0, length) for axis, length in enumerate(drawn.shape)]
    main_axis = drawn.shape.index(max(drawn.shape))
    neighbour = place[:main_axis] + [(place[main_axis] + 1) % drawn.shape[main_axis]] + place[main_axis + 1:]
    return drawn.at[tuple(place)].set(low).at[tuple(neighbour)].set(top_value)


def level_of(own_key, extent, cuts, low, high):
    gain, own = 1.0, jax.random.fold_in(own_key, 6)
    for axis_at, parts in cuts:
        draws = jnp.exp(jax.random.uniform(jax.random.fold_in(own, axis_at), (parts,), jnp.float32, low / len(cuts), high / len(cuts)))
        gain = gain * jnp.repeat(draws, extent[axis_at] // parts).reshape([-1 if axis == axis_at else 1 for axis in range(len(extent))])
    return gain


def scatter_about(rng, extent, deviation, most, cuts=(), held_as=jnp.bfloat16):
    entries = deviation * jax.random.normal(rng, extent, jnp.float32)
    if cuts:
        entries = entries * level_of(rng, extent, cuts, -0.22, 0.18)
    return jnp.clip(entries, -most, most).astype(held_as)


def setup_inputs(seed: int = 0) -> dict:
    key_list = jax.random.split(jax.random.key(seed), 7)
    return {
        "orbitals": draw_orbitals(jax.random.fold_in(key_list[6], 71), 0),
        "potential": jnp.clip(-2.0 + 3.0 * jax.random.uniform(key_list[1], (NX, NY, NZ), jnp.float32) ** level_of(key_list[1], (NX, NY, NZ), ((0, 8),), -0.2, 0.2), -2.0, 1.0),
        "projectors": scatter_about(key_list[2], (NPROJ, N_GRID * ENT), 0.3, 3.0, ((1, 8),), jnp.float32),
        "coupling": scatter_about(key_list[3], (NATOM, NPROJ, NPROJ), 1.0, 4.0, ((0, 8),), jnp.float32),
        "entry_cell": place_ends(jax.random.randint(key_list[4], (N_GRID * ENT,), 0, CX * NY * NZ), jax.random.fold_in(key_list[4], 1), 0, (CX * NY * NZ) - 1).astype(jnp.int32),
        "entry_atom": draw_entry_atom(jax.random.fold_in(key_list[6], 71), 0),
    }


CENTER = 34.0
HALF = 30.0
SPACING = 0.5
REACH = 6

def stencil_weights():
    factorial_of = math.factorial
    side_weights = [2.0 * (-1.0) ** (k + 1) * factorial_of(REACH) ** 2 / (k * k * factorial_of(REACH - k) * factorial_of(REACH + k)) for k in range(1, REACH + 1)]
    return (-2.0 * sum(side_weights), side_weights)

def kinetic(padded, shape):
    center, side_weights = stencil_weights()
    size_x, size_y, size_z = (shape[1], shape[2], shape[3])
    inner = padded[:, REACH:REACH + size_x, REACH:REACH + size_y, REACH:REACH + size_z]
    total = 3.0 * center * inner
    for k in range(1, REACH + 1):
        weight = side_weights[k - 1]
        plus_x = padded[:, REACH + k:REACH + k + size_x, REACH:REACH + size_y, REACH:REACH + size_z]
        minus_x = padded[:, REACH - k:REACH - k + size_x, REACH:REACH + size_y, REACH:REACH + size_z]
        plus_y = padded[:, REACH:REACH + size_x, REACH + k:REACH + k + size_y, REACH:REACH + size_z]
        minus_y = padded[:, REACH:REACH + size_x, REACH - k:REACH - k + size_y, REACH:REACH + size_z]
        plus_z = padded[:, REACH:REACH + size_x, REACH:REACH + size_y, REACH + k:REACH + k + size_z]
        minus_z = padded[:, REACH:REACH + size_x, REACH:REACH + size_y, REACH - k:REACH - k + size_z]
        total = total + weight * (plus_x + minus_x + plus_y + minus_y + plus_z + minus_z)
    return -0.5 / (SPACING * SPACING) * total

def nonlocal_term(flat_field, projectors, coupling, entry_cell, entry_atom):
    highest = lax.Precision.HIGHEST
    count = flat_field.shape[0]
    cell_index = entry_cell.reshape(N_GRID, ENT)
    atom_index = entry_atom.reshape(N_GRID, ENT)
    projector_values = projectors.reshape(NPROJ, N_GRID, ENT)
    values = jnp.take_along_axis(flat_field, jnp.broadcast_to(cell_index[None], (count, N_GRID, ENT)), axis=2)
    onehot = (atom_index[:, :, None] == jnp.arange(N_GRID * ATOM_DEV, dtype=jnp.int32)[None, None, :]).astype(jnp.float32)
    weighted = projector_values[:, None] * values[None]
    projector_coeffs = jnp.einsum('jbge,gea->ajb', weighted, onehot, precision=highest)
    mixed_coeffs = jnp.einsum('aij,ajb->aib', coupling, projector_coeffs, precision=highest)
    picked = jnp.einsum('gea,aib->ibge', onehot, mixed_coeffs, precision=highest)
    back_values = jnp.sum(projector_values[:, None] * picked, axis=0)
    domain_index = jnp.broadcast_to(jnp.arange(N_GRID, dtype=jnp.int32)[:, None], (N_GRID, ENT))
    result = jnp.zeros(flat_field.shape, jnp.float32)
    return result.at[:, domain_index, cell_index].add(back_values)

def apply_hamiltonian(group, potential, projectors, coupling, entry_cell, entry_atom):
    padded = jnp.pad(group, ((0, 0), (REACH, REACH), (REACH, REACH), (REACH, REACH)))
    kinetic_part = kinetic(padded, group.shape)
    flat_field = group.reshape(group.shape[0], N_GRID, CX * NY * NZ)
    nonlocal_part = nonlocal_term(flat_field, projectors, coupling, entry_cell, entry_atom).reshape(group.shape)
    return kinetic_part + potential[None] * group + nonlocal_part

def reference(orbitals, potential, projectors, coupling, entry_cell, entry_atom):
    highest = lax.Precision.HIGHEST

    def filter_group(group):
        first = apply_hamiltonian(group, potential, projectors, coupling, entry_cell, entry_atom)
        filtered_one = (first - CENTER * group) / HALF
        second = apply_hamiltonian(filtered_one, potential, projectors, coupling, entry_cell, entry_atom)
        return 2.0 * (second - CENTER * filtered_one) / HALF - group
    grouped = orbitals.reshape(N_BAND, ORB_DEV, NX, NY, NZ)
    filtered = lax.map(filter_group, grouped)
    cell_total = NX * NY * NZ
    flat_field = filtered.reshape(NORB, cell_total)
    panel = flat_field[:ORB_DEV]
    gram_matrix = jnp.dot(panel.astype(jnp.float32), panel.T.astype(jnp.float32), precision=highest, preferred_element_type=jnp.float32) / cell_total
    factor_lower = jnp.linalg.cholesky(gram_matrix)
    panel_basis = jax.scipy.linalg.solve_triangular(factor_lower, panel, lower=True)
    others = flat_field[ORB_DEV:]
    correlations = jnp.dot(panel_basis.astype(jnp.float32), others.T.astype(jnp.float32), precision=highest, preferred_element_type=jnp.float32) / cell_total
    others = others - jnp.dot(correlations.T.astype(jnp.float32), panel_basis.astype(jnp.float32), precision=highest, preferred_element_type=jnp.float32)
    return jnp.concatenate([panel_basis, others], axis=0).reshape(orbitals.shape)
```

```python
import functools
import math

import jax
import jax.numpy as jnp
from jax import lax
from jax.experimental import pallas as pl
from jax.experimental.pallas import tpu as pltpu
from jax.sharding import PartitionSpec as P

CENTER = 34.0
HALF = 30.0
SPACING = 0.5
REACH = 6
LANES = 128
ATOM_DEV = 8
GROUP = 32
TILE = 256
MESH = pl.DeviceIdType.MESH
COEF_STEPS = (-2, -1, 1, 2)


def stencil_weights():
    fact = math.factorial
    side = [
        2.0 * (-1.0) ** (k + 1) * fact(REACH) ** 2 / (k * k * fact(REACH - k) * fact(REACH + k))
        for k in range(1, REACH + 1)
    ]
    return -2.0 * sum(side), side


C0, CK = stencil_weights()
KIN = -0.5 / (SPACING * SPACING)
DIAG = (3.0 * KIN * C0 - CENTER) / HALF
EK = [KIN * c / HALF for c in CK]


def split(x):
    high = x.astype(jnp.bfloat16)
    return high, (x - high.astype(jnp.float32)).astype(jnp.bfloat16)


def dot(a, b):
    return jnp.dot(a, b, preferred_element_type=jnp.float32)


def kernel(
    n_band, n_grid, nx, ny, ent,
    orb_ref, pot_ref, proj_ref, cp_ref, cell_ref, atom_ref,
    out_ref,
    ext1, ext2, filt, panel, rows_m, rows_t, lane_m, m_row, m_col, picked, spread, vcat, acc,
    zmat, wcat, cols, coef_out, coef_in, coup_in, pairs, gram_out, gram_in,
    own_sem, halo_send, halo_recv, coef_send, coef_recv, coup_send, coup_recv,
    scat_send, scat_recv, gath_send, gath_recv, sib_send, sib_recv, copy_sem,
    gram_send, gram_recv,
):
    f32, bf16 = jnp.float32, jnp.bfloat16
    norb = orb_ref.shape[0]
    plane_rows = nx * ny
    reach_rows = REACH * ny
    chips = n_band // 2
    piece = plane_rows // chips
    band, grid = lax.axis_index("band"), lax.axis_index("grid")
    chip = lax.div(band, 2)
    core = lax.rem(band, 2)
    sibling = band + 1 - 2 * core
    main = core == 0
    has_left, has_right = grid > 0, grid < n_grid - 1

    def peer(step):
        return lax.rem(grid + step + n_grid, n_grid)

    barrier = pltpu.get_barrier_semaphore()
    for step in range(1, n_grid):
        pl.semaphore_signal(barrier, inc=1, device_id=(band, peer(step)), device_id_type=MESH)
    pl.semaphore_signal(barrier, inc=1, device_id=(sibling, grid), device_id_type=MESH)

    def other_chip(step):
        return 2 * lax.rem(chip + step, chips)

    @pl.when(main)
    def _():
        @pl.loop(1, chips)
        def _(step):
            pl.semaphore_signal(
                barrier, inc=1, device_id=(other_chip(step), grid), device_id_type=MESH
            )

        pl.semaphore_wait(barrier, n_grid + chips - 1)

    @pl.when(core == 1)
    def _():
        pl.semaphore_wait(barrier, n_grid)

    def halo(source, start, ext, b, app, side):
        step = -1 if side == 0 else 1
        first = start if side == 0 else start + plane_rows - reach_rows
        land = reach_rows + plane_rows if side == 0 else 0
        return pltpu.make_async_remote_copy(
            src_ref=source.at[b, pl.ds(first, reach_rows)],
            dst_ref=ext.at[b, pl.ds(land, reach_rows)],
            send_sem=halo_send.at[app, b, side],
            recv_sem=halo_recv.at[app, b, 1 - side],
            device_id=(band, grid + step),
            device_id_type=MESH,
        )

    def halo_source(app):
        return (orb_ref, 0, ext1) if app == 0 else (ext2, reach_rows, ext2)

    def send_halos(b, app):
        source, start, ext = halo_source(app)

        @pl.when(has_left)
        def _():
            halo(source, start, ext, b, app, 0).start()

        @pl.when(has_right)
        def _():
            halo(source, start, ext, b, app, 1).start()

    def wait_halos(b, app, sent):
        source, start, ext = halo_source(app)

        @pl.when(has_left)
        def _():
            if sent:
                halo(source, start, ext, b, app, 0).wait_send()
            else:
                halo(source, start, ext, b, app, 1).wait_recv()

        @pl.when(has_right)
        def _():
            if sent:
                halo(source, start, ext, b, app, 1).wait_send()
            else:
                halo(source, start, ext, b, app, 0).wait_recv()

    def own_copy(b):
        return pltpu.make_async_copy(
            orb_ref.at[b], ext1.at[b, pl.ds(reach_rows, plane_rows)], own_sem.at[b]
        )

    @pl.loop(0, norb)
    def _(b):
        send_halos(b, 0)
        own_copy(b).start()

    def coup_copy(k):
        return pltpu.make_async_remote_copy(
            src_ref=cp_ref, dst_ref=coup_in.at[k],
            send_sem=coup_send.at[k], recv_sem=coup_recv.at[k],
            device_id=(band, peer((-1, 1)[k])), device_id_type=MESH,
        )

    for k in range(2):
        coup_copy(k).start()

    zero_halo = jnp.zeros((norb, reach_rows, LANES), f32)
    for ext in (ext1, ext2):
        @pl.when(jnp.logical_not(has_left))
        def _():
            ext[:, 0:reach_rows] = zero_halo

        @pl.when(jnp.logical_not(has_right))
        def _():
            ext[:, reach_rows + plane_rows :] = zero_halo

    cell = cell_ref[...]
    atom = atom_ref[...]
    row_of = lax.shift_right_logical(cell, 7)
    lane_of = jnp.bitwise_and(cell, LANES - 1)
    near = jnp.where(atom >= 0, atom - (grid - 1) * ATOM_DEV, -1000)
    for j in range(4):
        hit = lax.broadcasted_iota(jnp.int32, (GROUP, ent), 0) == near
        high, low = split(jnp.where(hit, proj_ref[j : j + 1, :], 0.0))
        m_row[GROUP * j : GROUP * (j + 1)] = high
        m_row[LANES + GROUP * j : LANES + GROUP * (j + 1)] = low
    packed = jnp.concatenate(
        [row_of.astype(f32), lane_of.astype(f32), near.astype(f32), near.astype(f32), proj_ref[...]],
        axis=0,
    )
    cols[...] = packed.T

    @pl.loop(0, ent // TILE)
    def _(i):
        part = pl.ds(pl.multiple_of(i * TILE, TILE), TILE)
        column = cols[part, :]
        lane = lax.broadcasted_iota(jnp.int32, (TILE, LANES), 1).astype(f32)
        wide = lax.broadcasted_iota(jnp.int32, (TILE, plane_rows), 1).astype(f32)
        rows_m[part, :] = jnp.where(column[:, 0:1] == wide, 1.0, 0.0).astype(bf16)
        lane_m[part, :] = jnp.where(column[:, 1:2] == lane, 1.0, 0.0)
        total = jnp.zeros((TILE, LANES), f32)
        for j in range(4):
            total = jnp.where(column[:, 2:3] + (GROUP * j) == lane, column[:, 4 + j : 5 + j], total)
        high, low = split(total)
        m_col[part, 0:LANES] = high
        m_col[part, LANES:] = low

    @pl.loop(0, nx)
    def _(x):
        first = pl.multiple_of(x * ny, ny)
        down = lax.broadcasted_iota(jnp.int32, (ny, ent), 0) + first
        rows_t[pl.ds(first, ny), :] = jnp.where(down == row_of, 1.0, 0.0).astype(bf16)

    apart = jnp.abs(
        lax.broadcasted_iota(jnp.int32, (LANES, LANES), 0)
        - lax.broadcasted_iota(jnp.int32, (LANES, LANES), 1)
    )
    band_m = jnp.zeros((LANES, LANES), f32)
    for k in range(1, REACH + 1):
        band_m = jnp.where(apart == k, EK[k - 1], band_m)
    high, low = split(band_m)
    zmat[0:LANES, 0:LANES] = high
    zmat[0:LANES, LANES:] = low
    zmat[LANES:, 0:LANES] = high
    zmat[LANES:, LANES:] = jnp.zeros((LANES, LANES), bf16)

    def coef_copy(app, b, d):
        return pltpu.make_async_remote_copy(
            src_ref=coef_out.at[app, b], dst_ref=coef_in.at[app, b, d],
            send_sem=coef_send.at[app, b, d], recv_sem=coef_recv.at[app, b, d],
            device_id=(band, peer(COEF_STEPS[d])), device_id_type=MESH,
        )

    def cut(ext, b):
        for x in range(nx):
            high, low = split(ext[b, reach_rows + x * ny : reach_rows + (x + 1) * ny, :])
            vcat[b, x * ny : (x + 1) * ny, 0:LANES] = high
            vcat[b, x * ny : (x + 1) * ny, LANES:] = low

    def coefficients(ext, b, app):
        cut(ext, b)

        @pl.loop(0, ent // TILE)
        def _(i):
            part = pl.ds(pl.multiple_of(i * TILE, TILE), TILE)
            got = dot(rows_m[part, :], vcat[b])
            mask = lane_m[part, :]
            picked[part, 0:LANES] = (got[:, 0:LANES] * mask).astype(bf16)
            picked[part, LANES:] = (got[:, LANES:] * mask).astype(bf16)

        both = dot(m_row[...], picked[...])
        both = both[0:LANES] + both[LANES:]
        both = (both[:, 0:LANES] + both[:, LANES:]).T
        coef_out[app, b] = jnp.sum(both.reshape(LANES // 8, 8, LANES), axis=0)
        for d in range(len(COEF_STEPS)):
            coef_copy(app, b, d).start()

    lane8 = lax.broadcasted_iota(jnp.int32, (8, LANES), 1)
    slot8 = jnp.bitwise_and(lax.shift_right_logical(lane8, 3), 3)

    def near_total(app, b):
        total = coef_out[app, b]
        for d, step in enumerate(COEF_STEPS):
            coef_copy(app, b, d).wait_recv()
            shift = -step
            there = grid + shift
            lands = slot8 + shift
            keep = (slot8 < 3) & (lands >= 0) & (lands < 3) & (there >= 0) & (there < n_grid)
            total = total + pltpu.roll(
                jnp.where(keep, coef_in[app, b, d], 0.0), (8 * shift) % LANES, 1
            )
        return jnp.broadcast_to(jnp.sum(total, axis=0, keepdims=True), (8, LANES))

    def coupling_rows():
        total = cp_ref[...]
        for k, step in enumerate((-1, 1)):
            shift = -step
            there = grid + shift
            keep = (there >= 0) & (there < n_grid)
            total = total + pltpu.roll(
                jnp.where(keep, coup_in[k], 0.0), (8 * shift) % LANES, 1
            )
        return total

    def inner_terms(ext, b, app):
        near_c = near_total(app, b)
        mix = coupling_rows()
        mixed = jnp.zeros((8, LANES), f32)
        for k in range(4):
            turned = near_c if k == 0 else pltpu.roll(near_c, LANES - GROUP * k, 1)
            mixed = mixed + jnp.broadcast_to(mix[k : k + 1], (8, LANES)) * turned
        high, low = split(jnp.broadcast_to(mixed[0:1] * (1.0 / HALF), (LANES, LANES)))
        wcat[0:LANES, 0:LANES] = high
        wcat[0:LANES, LANES:] = high
        wcat[LANES:, 0:LANES] = low
        wcat[LANES:, LANES:] = jnp.zeros((LANES, LANES), bf16)

        @pl.loop(0, ent // TILE)
        def _(i):
            part = pl.ds(pl.multiple_of(i * TILE, TILE), TILE)
            back = lax.dot_general(
                m_col[part, :], wcat[...], (((1,), (1,)), ((), ())), preferred_element_type=f32
            )
            high, low = split((back[:, 0:LANES] + back[:, LANES:]) * lane_m[part, :])
            spread[part, 0:LANES] = high
            spread[part, LANES:] = low

        step = 2 * ny

        @pl.loop(0, plane_rows // step)
        def _(i):
            part = pl.ds(pl.multiple_of(i * step, step), step)
            both = dot(rows_t[part, :], spread[...]) + dot(vcat[b, part, :], zmat[...])
            acc[part, :] = both[:, 0:LANES] + both[:, LANES:]

        row = lax.broadcasted_iota(jnp.int32, (ny, LANES), 0)

        @pl.loop(0, nx)
        def _(x):
            first = pl.multiple_of(x * ny, ny)
            cells = ext[b, pl.ds(pl.multiple_of(reach_rows + first, ny), ny), :]
            total = acc[pl.ds(first, ny), :]
            for k in range(1, REACH + 1):
                before = jnp.where(row >= k, pltpu.roll(cells, k, 0), 0.0)
                after = jnp.where(row < ny - k, pltpu.roll(cells, ny - k, 0), 0.0)
                total = total + EK[k - 1] * (before + after)
            acc[pl.ds(first, ny), :] = total

    def along_x(ext, b, store):
        @pl.loop(0, ny // 8)
        def _(t):
            first = pl.multiple_of(t * 8, 8)
            cells = [
                ext[b, pl.ds(pl.multiple_of(x * ny + first, 8), 8), :]
                for x in range(nx + 2 * REACH)
            ]
            for x in range(nx):
                place = pl.ds(pl.multiple_of(x * ny + first, 8), 8)
                here = cells[x + REACH]
                total = acc[place, :] + here * (pot_ref[place, :] * (1.0 / HALF) + DIAG)
                for k in range(1, REACH + 1):
                    total = total + EK[k - 1] * (cells[x + REACH + k] + cells[x + REACH - k])
                store(x, first, place, total)

    @pl.loop(0, norb)
    def _(b):
        own_copy(b).wait()
        coefficients(ext1, b, 0)

    for k in range(2):
        coup_copy(k).wait_recv()

    @pl.loop(0, norb)
    def _(b):
        inner_terms(ext1, b, 0)
        wait_halos(b, 0, False)

        def store(x, first, place, total):
            ext2[b, pl.ds(pl.multiple_of(reach_rows + x * ny + first, 8), 8), :] = total

        along_x(ext1, b, store)
        send_halos(b, 1)
        coefficients(ext2, b, 1)

    def scatter_copy(b, to):
        part = pl.ds(pl.multiple_of(to * piece, 8), piece)
        return pltpu.make_async_remote_copy(
            src_ref=filt.at[b, part], dst_ref=panel.at[b, part],
            send_sem=scat_send.at[b, to], recv_sem=scat_recv.at[b],
            device_id=(2 * to, grid), device_id_type=MESH,
        )

    def gather_copy(b, step):
        part = pl.ds(pl.multiple_of(chip * piece, 8), piece)
        return pltpu.make_async_remote_copy(
            src_ref=panel.at[b, part], dst_ref=panel.at[b, part],
            send_sem=gath_send.at[b, step], recv_sem=gath_recv.at[b],
            device_id=(other_chip(step), grid), device_id_type=MESH,
        )

    def sibling_copy(b):
        return pltpu.make_async_remote_copy(
            src_ref=panel.at[b], dst_ref=panel.at[b],
            send_sem=sib_send.at[b], recv_sem=sib_recv.at[b],
            device_id=(sibling, grid), device_id_type=MESH,
        )

    def self_copy(b):
        return pltpu.make_async_copy(filt.at[b], panel.at[b], copy_sem.at[b])

    root = band == 0
    follower = main & jnp.logical_not(root)

    def phase_scatter(b):
        @pl.when(root)
        def _():
            @pl.loop(1, chips)
            def _(to):
                scatter_copy(b, to).start()

            self_copy(b).start()

    def phase_gather(b):
        @pl.when(root)
        def _():
            self_copy(b).wait()

        @pl.when(follower)
        def _():
            scatter_copy(b, chip).wait_recv()

        @pl.when(main)
        def _():
            @pl.loop(1, chips)
            def _(step):
                @pl.when(other_chip(step) != 0)
                def _():
                    gather_copy(b, step).start()

    def phase_sibling(b):
        @pl.when(follower)
        def _():
            most = panel.at[b, pl.ds(0, (chips - 1) * piece)]
            pltpu.make_async_copy(most, most, gath_recv.at[b]).wait()

        @pl.when(main)
        def _():
            sibling_copy(b).start()

    def phase_last(b):
        @pl.when(core == 1)
        def _():
            sibling_copy(b).wait_recv()

    @pl.loop(0, norb)
    def _(b):
        inner_terms(ext2, b, 1)
        wait_halos(b, 1, False)

        def store(x, first, place, total):
            before = ext1[b, pl.ds(pl.multiple_of(reach_rows + x * ny + first, 8), 8), :]
            filt[b, place, :] = 2.0 * total - before

        along_x(ext2, b, store)
        phase_scatter(b)

        @pl.when(b >= 1)
        def _():
            phase_gather(b - 1)

        @pl.when(b >= 2)
        def _():
            phase_sibling(b - 2)

    phase_gather(norb - 1)
    phase_sibling(norb - 2)
    phase_sibling(norb - 1)
    for b in range(norb):
        phase_last(b)

    couples = [(k, m) for k in range(norb) for m in range(k + 1)]
    n_pairs = len(couples) + norb * norb

    def add_pairs(t, sums):
        place = pl.ds(pl.multiple_of(t * 8, 8), 8)
        p = [panel[k, place, :] for k in range(norb)]
        f = [filt[n, place, :] for n in range(norb)]
        terms = [p[k] * p[m] for k, m in couples] + [p[k] * f[n] for k in range(norb) for n in range(norb)]
        return tuple(s + term for s, term in zip(sums, terms))

    sums = lax.fori_loop(
        0, plane_rows // 8, add_pairs, tuple(jnp.zeros((8, LANES), f32) for _ in range(n_pairs))
    )
    pairs[...] = jnp.zeros(pairs.shape, f32)
    for i, s in enumerate(sums):
        pairs[i : i + 1, :] = jnp.sum(s, axis=0, keepdims=True)
    gram_out[...] = jnp.sum(pairs[...].T.reshape(LANES // 8, 8, LANES), axis=0)

    def gram_copy(step):
        return pltpu.make_async_remote_copy(
            src_ref=gram_out, dst_ref=gram_in.at[step],
            send_sem=gram_send.at[step], recv_sem=gram_recv.at[step],
            device_id=(band, peer(step)), device_id_type=MESH,
        )

    for step in range(1, n_grid):
        gram_copy(step).start()
    total = gram_out[...]
    for step in range(1, n_grid):
        gram_copy(step).wait_recv()
        total = total + gram_in[step]
    total = jnp.sum(total, axis=0, keepdims=True) * (1.0 / (plane_rows * LANES * n_grid))
    lane1 = lax.broadcasted_iota(jnp.int32, (1, LANES), 1)

    def number(i):
        one = jnp.sum(jnp.where(lane1 == i, total, 0.0), axis=1, keepdims=True)
        return jnp.broadcast_to(one, (8, LANES))

    gram = {couple: number(i) for i, couple in enumerate(couples)}
    raw = [[number(len(couples) + k * norb + n) for n in range(norb)] for k in range(norb)]
    lower, inverse = {}, {}
    for j in range(norb):
        left = gram[j, j]
        for m in range(j):
            left = left - lower[j, m] * lower[j, m]
        lower[j, j] = jnp.sqrt(left)
        inverse[j, j] = 1.0 / lower[j, j]
        for i in range(j + 1, norb):
            left = gram[i, j]
            for m in range(j):
                left = left - lower[i, m] * lower[j, m]
            lower[i, j] = left * inverse[j, j]
    for j in range(norb):
        for i in range(j + 1, norb):
            left = lower[i, j] * inverse[j, j]
            for m in range(j + 1, i):
                left = left + lower[i, m] * inverse[m, j]
            inverse[i, j] = -left * inverse[i, i]
    corr = [
        [sum(inverse[k, m] * raw[m][n] for m in range(k + 1)) for n in range(norb)]
        for k in range(norb)
    ]
    weight = [[None] * norb for _ in range(norb)]
    zero8 = jnp.zeros((8, LANES), f32)
    for m in range(norb):
        for n in range(norb):
            away = -sum(inverse[k, m] * corr[k][n] for k in range(m, norb))
            weight[m][n] = jnp.where(root, inverse[n, m] if m <= n else zero8, away)
    keep = jnp.where(root, zero8, jnp.ones((8, LANES), f32))

    @pl.loop(0, plane_rows // 8)
    def _(t):
        place = pl.ds(pl.multiple_of(t * 8, 8), 8)
        p = [panel[k, place, :] for k in range(norb)]
        for n in range(norb):
            value = keep * filt[n, place, :]
            for m in range(norb):
                value = value + weight[m][n] * p[m]
            out_ref[n, place, :] = value

    @pl.loop(0, norb)
    def _(b):
        wait_halos(b, 0, True)
        wait_halos(b, 1, True)
        for app in range(2):
            for d in range(len(COEF_STEPS)):
                coef_copy(app, b, d).wait_send()

        @pl.when(root)
        def _():
            @pl.loop(1, chips)
            def _(to):
                scatter_copy(b, to).wait_send()

        @pl.when(main)
        def _():
            @pl.loop(1, chips)
            def _(step):
                @pl.when(other_chip(step) != 0)
                def _():
                    gather_copy(b, step).wait_send()

            sibling_copy(b).wait_send()

    for k in range(2):
        coup_copy(k).wait_send()
    for step in range(1, n_grid):
        gram_copy(step).wait_send()


def local(n_band, n_grid, orbitals, potential, projectors, coupling, entry_cell, entry_atom):
    norb, nx, ny, nz = orbitals.shape
    ent = entry_cell.shape[0]
    rows = nx * ny
    chips = n_band // 2
    f32, bf16 = jnp.float32, jnp.bfloat16
    turned = jnp.stack(
        [
            jnp.stack([coupling[:, i, (i + k) % 4] for i in range(4)], axis=0)
            for k in range(4)
        ],
        axis=0,
    )
    mix = jnp.pad(turned, ((0, 4), (0, 0), (ATOM_DEV, GROUP - 2 * ATOM_DEV))).reshape(8, LANES)
    vmem, dma = pltpu.VMEM, pltpu.SemaphoreType.DMA
    ext_rows = rows + 2 * REACH * ny
    whole = pl.BlockSpec(memory_space=pltpu.VMEM)
    out = pl.pallas_call(
        functools.partial(kernel, n_band, n_grid, nx, ny, ent),
        out_shape=jax.ShapeDtypeStruct((norb, rows, nz), f32),
        in_specs=[pl.BlockSpec(memory_space=pl.ANY)] + [whole] * 5,
        out_specs=whole,
        scratch_shapes=[
            vmem((norb, ext_rows, nz), f32),
            vmem((norb, ext_rows, nz), f32),
            vmem((norb, rows, nz), f32),
            vmem((norb, rows, nz), f32),
            vmem((ent, rows), bf16),
            vmem((rows, ent), bf16),
            vmem((ent, LANES), f32),
            vmem((2 * LANES, ent), bf16),
            vmem((ent, 2 * LANES), bf16),
            vmem((ent, 2 * LANES), bf16),
            vmem((ent, 2 * LANES), bf16),
            vmem((norb, rows, 2 * LANES), bf16),
            vmem((rows, LANES), f32),
            vmem((2 * LANES, 2 * LANES), bf16),
            vmem((2 * LANES, 2 * LANES), bf16),
            vmem((ent, 8), f32),
            vmem((2, norb, 8, LANES), f32),
            vmem((2, norb, 4, 8, LANES), f32),
            vmem((2, 8, LANES), f32),
            vmem((LANES, LANES), f32),
            vmem((8, LANES), f32),
            vmem((n_grid, 8, LANES), f32),
            dma((norb,)),
            dma((2, norb, 2)), dma((2, norb, 2)),
            dma((2, norb, 4)), dma((2, norb, 4)),
            dma((2,)), dma((2,)),
            dma((norb, chips)), dma((norb,)),
            dma((norb, chips)), dma((norb,)),
            dma((norb,)), dma((norb,)),
            dma((norb,)),
            dma((n_grid,)), dma((n_grid,)),
        ],
        compiler_params=pltpu.CompilerParams(
            collective_id=0, has_side_effects=True, vmem_limit_bytes=48 * 1024 * 1024
        ),
        name="filter_panel",
    )(
        orbitals.reshape(norb, rows, nz),
        potential.reshape(rows, nz),
        projectors,
        mix,
        entry_cell.reshape(1, ent),
        entry_atom.reshape(1, ent),
    )
    return out.reshape(orbitals.shape)


def solution(mesh):
    return jax.shard_map(
        functools.partial(local, mesh.shape["band"], mesh.shape["grid"]),
        mesh=mesh,
        in_specs=(
            P("band", "grid", None, None),
            P("grid", None, None),
            P(None, "grid"),
            P("grid", None, None),
            P("grid"),
            P("grid"),
        ),
        out_specs=P("band", "grid", None, None),
        check_vma=False,
    )
```

```python
import functools
import math

import jax
import jax.numpy as jnp
from jax import lax
from jax.experimental import pallas as pl
from jax.experimental.pallas import tpu as pltpu
from jax.sharding import PartitionSpec as P

CENTER = 34.0
HALF = 30.0
SPACING = 0.5
REACH = 6
LANES = 128
ATOM_DEV = 8
GROUP = 32
TILE = 256
WIDE = 512
MESH = pl.DeviceIdType.MESH
COEF_STEPS = (-2, -1, 1, 2)


def stencil_weights():
    fact = math.factorial
    side = [
        2.0 * (-1.0) ** (k + 1) * fact(REACH) ** 2 / (k * k * fact(REACH - k) * fact(REACH + k))
        for k in range(1, REACH + 1)
    ]
    return -2.0 * sum(side), side


C0, CK = stencil_weights()
KIN = -0.5 / (SPACING * SPACING)
DIAG = (3.0 * KIN * C0 - CENTER) / HALF
EK = [KIN * c / HALF for c in CK]


def split(x):
    high = x.astype(jnp.bfloat16)
    return high, (x - high.astype(jnp.float32)).astype(jnp.bfloat16)


def dot(a, b):
    return jnp.dot(a, b, preferred_element_type=jnp.float32)


def kernel(
    n_band, n_grid, nx, ny, ent,
    orb_ref, pot_hbm, proj_hbm, coup_hbm, cell_hbm, atom_hbm,
    out_ref,
    pot_ref, proj_ref, coup_ref, cell_ref, atom_ref,
    ext1, ext2, filt, panel, rows_m, rows_t, lane_m, m_row, m_col, picked, spread, vcat, acc,
    zmat, wcat, cols, coef_out, coef_in, coup_own, coup_in, mix, pairs, gram_out, gram_in,
    load_sem, own_sem, halo_send, halo_recv, coef_send, coef_recv, coup_send, coup_recv,
    scat_send, scat_recv, z_send, z_recv, y_send, y_recv, sib_send, sib_recv, copy_sem,
    gram_send, gram_recv,
):
    f32, bf16 = jnp.float32, jnp.bfloat16
    norb = orb_ref.shape[0]
    plane_rows = nx * ny
    reach_rows = REACH * ny
    chips = n_band // 2
    n_zh = 4 if chips % 4 == 0 else 1
    n_y = chips // n_zh
    piece = plane_rows // chips
    share = piece * n_zh
    band, grid = lax.axis_index("band"), lax.axis_index("grid")
    chip = lax.div(band, 2)
    zh, yy = lax.rem(chip, n_zh), lax.div(chip, n_zh)
    core = lax.rem(band, 2)
    sibling = band + 1 - 2 * core
    main = core == 0
    has_left, has_right = grid > 0, grid < n_grid - 1

    def peer(step):
        return lax.rem(grid + step + n_grid, n_grid)

    loads = [
        pltpu.make_async_copy(source, there, load_sem.at[i])
        for i, (source, there) in enumerate(
            [
                (cell_hbm, cell_ref), (atom_hbm, atom_ref), (proj_hbm, proj_ref),
                (coup_hbm, coup_ref), (pot_hbm, pot_ref),
            ]
        )
    ]
    for load in loads:
        load.start()

    barrier = pltpu.get_barrier_semaphore()
    for step in range(1, n_grid):
        pl.semaphore_signal(barrier, inc=1, device_id=(band, peer(step)), device_id_type=MESH)
    pl.semaphore_signal(barrier, inc=1, device_id=(sibling, grid), device_id_type=MESH)

    def along_z(step):
        return 2 * (yy * n_zh + lax.rem(zh + step, n_zh))

    def along_y(step):
        return 2 * (lax.rem(yy + step, n_y) * n_zh + zh)

    root = band == 0
    follower = main & jnp.logical_not(root)
    crossed = (zh > 0) & (yy > 0)

    @pl.when(main)
    def _():
        for step in range(1, n_zh):
            pl.semaphore_signal(
                barrier, inc=1, device_id=(along_z(step), grid), device_id_type=MESH
            )
        for step in range(1, n_y):
            pl.semaphore_signal(
                barrier, inc=1, device_id=(along_y(step), grid), device_id_type=MESH
            )

        @pl.when(crossed)
        def _():
            pl.semaphore_signal(barrier, inc=1, device_id=(0, grid), device_id_type=MESH)

        @pl.when(root)
        def _():
            for y in range(1, n_y):
                for z in range(1, n_zh):
                    pl.semaphore_signal(
                        barrier, inc=1, device_id=(2 * (y * n_zh + z), grid), device_id_type=MESH
                    )

            pl.semaphore_wait(barrier, n_grid + chips - 1)

        @pl.when(crossed)
        def _():
            pl.semaphore_wait(barrier, n_grid + n_zh + n_y - 1)

        @pl.when(jnp.logical_not(crossed | root))
        def _():
            pl.semaphore_wait(barrier, n_grid + n_zh + n_y - 2)

    @pl.when(core == 1)
    def _():
        pl.semaphore_wait(barrier, n_grid)

    def halo(source, start, ext, b, app, side):
        step = -1 if side == 0 else 1
        first = start if side == 0 else start + plane_rows - reach_rows
        land = reach_rows + plane_rows if side == 0 else 0
        return pltpu.make_async_remote_copy(
            src_ref=source.at[b, pl.ds(first, reach_rows)],
            dst_ref=ext.at[b, pl.ds(land, reach_rows)],
            send_sem=halo_send.at[app, b, side],
            recv_sem=halo_recv.at[app, b, 1 - side],
            device_id=(band, grid + step),
            device_id_type=MESH,
        )

    def halo_source(app):
        return (orb_ref, 0, ext1) if app == 0 else (ext2, reach_rows, ext2)

    def send_halos(b, app):
        source, start, ext = halo_source(app)

        @pl.when(has_left)
        def _():
            halo(source, start, ext, b, app, 0).start()

        @pl.when(has_right)
        def _():
            halo(source, start, ext, b, app, 1).start()

    def wait_halos(b, app, sent):
        source, start, ext = halo_source(app)

        @pl.when(has_left)
        def _():
            if sent:
                halo(source, start, ext, b, app, 0).wait_send()
            else:
                halo(source, start, ext, b, app, 1).wait_recv()

        @pl.when(has_right)
        def _():
            if sent:
                halo(source, start, ext, b, app, 1).wait_send()
            else:
                halo(source, start, ext, b, app, 0).wait_recv()

    def own_copy(b):
        return pltpu.make_async_copy(
            orb_ref.at[b], ext1.at[b, pl.ds(reach_rows, plane_rows)], own_sem.at[b]
        )

    @pl.loop(0, norb)
    def _(b):
        send_halos(b, 0)
        own_copy(b).start()

    for load in loads[:4]:
        load.wait()
    coup_own[...] = jnp.zeros(coup_own.shape, f32)
    for i in range(4):
        first = GROUP * i + ATOM_DEV
        coup_own[0:4, first : first + ATOM_DEV] = coup_ref[i]

    def coup_copy(k):
        return pltpu.make_async_remote_copy(
            src_ref=coup_own, dst_ref=coup_in.at[k],
            send_sem=coup_send.at[k], recv_sem=coup_recv.at[k],
            device_id=(band, peer((-1, 1)[k])), device_id_type=MESH,
        )

    for k in range(2):
        coup_copy(k).start()

    zero_halo = jnp.zeros((norb, reach_rows, LANES), f32)
    for ext in (ext1, ext2):
        @pl.when(jnp.logical_not(has_left))
        def _():
            ext[:, 0:reach_rows] = zero_halo

        @pl.when(jnp.logical_not(has_right))
        def _():
            ext[:, reach_rows + plane_rows :] = zero_halo

    cell = cell_ref[...]
    atom = atom_ref[...]
    row_of = lax.shift_right_logical(cell, 7)
    lane_of = jnp.bitwise_and(cell, LANES - 1)
    near = jnp.where(atom >= 0, atom - (grid - 1) * ATOM_DEV, -1000)
    for j in range(4):
        hit = lax.broadcasted_iota(jnp.int32, (GROUP, ent), 0) == near
        high, low = split(jnp.where(hit, proj_ref[j : j + 1, :], 0.0))
        m_row[GROUP * j : GROUP * (j + 1)] = high
        m_row[LANES + GROUP * j : LANES + GROUP * (j + 1)] = low
    packed = jnp.concatenate(
        [row_of.astype(f32), lane_of.astype(f32), near.astype(f32), near.astype(f32), proj_ref[...]],
        axis=0,
    )
    cols[...] = packed.T

    @pl.loop(0, ent // TILE)
    def _(i):
        part = pl.ds(pl.multiple_of(i * TILE, TILE), TILE)
        column = cols[part, :]
        lane = lax.broadcasted_iota(jnp.int32, (TILE, LANES), 1).astype(f32)
        wide = lax.broadcasted_iota(jnp.int32, (TILE, plane_rows), 1).astype(f32)
        rows_m[part, :] = jnp.where(column[:, 0:1] == wide, 1.0, 0.0).astype(bf16)
        lane_m[part, :] = jnp.where(column[:, 1:2] == lane, 1.0, 0.0).astype(bf16)
        total = jnp.zeros((TILE, LANES), f32)
        for j in range(4):
            total = jnp.where(column[:, 2:3] + (GROUP * j) == lane, column[:, 4 + j : 5 + j], total)
        high, low = split(total)
        m_col[part, 0:LANES] = high
        m_col[part, LANES:] = low

    @pl.loop(0, nx)
    def _(x):
        first = pl.multiple_of(x * ny, ny)
        down = lax.broadcasted_iota(jnp.int32, (ny, ent), 0) + first
        rows_t[pl.ds(first, ny), :] = jnp.where(down == row_of, 1.0, 0.0).astype(bf16)

    apart = jnp.abs(
        lax.broadcasted_iota(jnp.int32, (LANES, LANES), 0)
        - lax.broadcasted_iota(jnp.int32, (LANES, LANES), 1)
    )
    band_m = jnp.zeros((LANES, LANES), f32)
    for k in range(1, REACH + 1):
        band_m = jnp.where(apart == k, EK[k - 1], band_m)
    high, low = split(band_m)
    zmat[0:LANES, 0:LANES] = high
    zmat[0:LANES, LANES:] = low
    zmat[LANES:, 0:LANES] = high
    zmat[LANES:, LANES:] = jnp.zeros((LANES, LANES), bf16)

    def coef_copy(app, b, d):
        return pltpu.make_async_remote_copy(
            src_ref=coef_out.at[app, b], dst_ref=coef_in.at[app, b, d],
            send_sem=coef_send.at[app, b, d], recv_sem=coef_recv.at[app, b, d],
            device_id=(band, peer(COEF_STEPS[d])), device_id_type=MESH,
        )

    def cut(ext, b):
        for x in range(nx):
            high, low = split(ext[b, reach_rows + x * ny : reach_rows + (x + 1) * ny, :])
            vcat[b, x * ny : (x + 1) * ny, 0:LANES] = high
            vcat[b, x * ny : (x + 1) * ny, LANES:] = low

    def coefficients(ext, b, app):
        cut(ext, b)

        for i in range(0, ent, WIDE):
            got = dot(rows_m[i : i + WIDE, :], vcat[b]).astype(bf16)
            mask = lane_m[i : i + WIDE, :]
            picked[i : i + WIDE, 0:LANES] = got[:, 0:LANES] * mask
            picked[i : i + WIDE, LANES:] = got[:, LANES:] * mask

        both = dot(m_row[...], picked[...])
        both = both[0:LANES] + both[LANES:]
        both = (both[:, 0:LANES] + both[:, LANES:]).T
        coef_out[app, b] = jnp.sum(both.reshape(LANES // 8, 8, LANES), axis=0)
        for d in range(len(COEF_STEPS)):
            coef_copy(app, b, d).start()

    lane8 = lax.broadcasted_iota(jnp.int32, (8, LANES), 1)
    slot8 = jnp.bitwise_and(lax.shift_right_logical(lane8, 3), 3)

    def near_total(app, b):
        total = coef_out[app, b]
        for d, step in enumerate(COEF_STEPS):
            coef_copy(app, b, d).wait_recv()
            shift = -step
            there = grid + shift
            lands = slot8 + shift
            keep = (slot8 < 3) & (lands >= 0) & (lands < 3) & (there >= 0) & (there < n_grid)
            total = total + pltpu.roll(
                jnp.where(keep, coef_in[app, b, d], 0.0), (8 * shift) % LANES, 1
            )
        return jnp.broadcast_to(jnp.sum(total, axis=0, keepdims=True), (8, LANES))

    def coupling_rows():
        total = coup_own[...]
        for k, step in enumerate((-1, 1)):
            coup_copy(k).wait_recv()
            shift = -step
            there = grid + shift
            keep = (there >= 0) & (there < n_grid)
            total = total + pltpu.roll(
                jnp.where(keep, coup_in[k], 0.0), (8 * shift) % LANES, 1
            )
        group = lax.shift_right_logical(lax.broadcasted_iota(jnp.int32, (1, LANES), 1), 5)
        for k in range(4):
            line = jnp.zeros((1, LANES), f32)
            for i in range(4):
                j = (i + k) % 4
                line = jnp.where(group == i, total[j : j + 1], line)
            mix[8 * k : 8 * k + 8, :] = jnp.broadcast_to(line * (1.0 / HALF), (8, LANES))

    def inner_terms(ext, b, app):
        near_c = near_total(app, b)
        mixed = mix[0:8, :] * near_c
        for k in range(1, 4):
            mixed = mixed + mix[8 * k : 8 * k + 8, :] * pltpu.roll(near_c, LANES - GROUP * k, 1)
        high, low = split(jnp.broadcast_to(mixed[0:1], (LANES, LANES)).T)
        wcat[0:LANES, 0:LANES] = high
        wcat[0:LANES, LANES:] = low
        wcat[LANES:, 0:LANES] = high
        wcat[LANES:, LANES:] = jnp.zeros((LANES, LANES), bf16)

        for i in range(0, ent, WIDE):
            back = dot(m_col[i : i + WIDE, :], wcat[...])
            high, low = split(back[:, 0:LANES] + back[:, LANES:])
            mask = lane_m[i : i + WIDE, :]
            spread[i : i + WIDE, 0:LANES] = high * mask
            spread[i : i + WIDE, LANES:] = low * mask

        step = 4 * ny

        for i in range(0, plane_rows, step):
            part = slice(i, i + step)
            both = dot(rows_t[part, :], spread[...]) + dot(vcat[b, part, :], zmat[...])
            acc[part, :] = both[:, 0:LANES] + both[:, LANES:]

        row = lax.broadcasted_iota(jnp.int32, (ny, LANES), 0)

        @pl.loop(0, nx)
        def _(x):
            first = pl.multiple_of(x * ny, ny)
            cells = ext[b, pl.ds(pl.multiple_of(reach_rows + first, ny), ny), :]
            total = acc[pl.ds(first, ny), :]
            for k in range(1, REACH + 1):
                before = jnp.where(row >= k, pltpu.roll(cells, k, 0), 0.0)
                after = jnp.where(row < ny - k, pltpu.roll(cells, ny - k, 0), 0.0)
                total = total + EK[k - 1] * (before + after)
            acc[pl.ds(first, ny), :] = total

    def along_x(ext, b, store):
        @pl.loop(0, ny // 8)
        def _(t):
            first = pl.multiple_of(t * 8, 8)
            cells = [
                ext[b, pl.ds(pl.multiple_of(x * ny + first, 8), 8), :]
                for x in range(nx + 2 * REACH)
            ]
            for x in range(nx):
                place = pl.ds(pl.multiple_of(x * ny + first, 8), 8)
                here = cells[x + REACH]
                total = acc[place, :] + here * (pot_ref[place, :] * (1.0 / HALF) + DIAG)
                for k in range(1, REACH + 1):
                    total = total + EK[k - 1] * (cells[x + REACH + k] + cells[x + REACH - k])
                store(x, first, place, total)

    @pl.loop(0, norb)
    def _(b):
        own_copy(b).wait()
        coefficients(ext1, b, 0)

    coupling_rows()
    loads[4].wait()

    @pl.loop(0, norb)
    def _(b):
        inner_terms(ext1, b, 0)
        wait_halos(b, 0, False)

        def store(x, first, place, total):
            ext2[b, pl.ds(pl.multiple_of(reach_rows + x * ny + first, 8), 8), :] = total

        along_x(ext1, b, store)
        send_halos(b, 1)
        coefficients(ext2, b, 1)

    def scatter_copy(b, to):
        part = pl.ds(pl.multiple_of(to * piece, 8), piece)
        return pltpu.make_async_remote_copy(
            src_ref=filt.at[b, part], dst_ref=panel.at[b, part],
            send_sem=scat_send.at[b, to], recv_sem=scat_recv.at[b],
            device_id=(2 * to, grid), device_id_type=MESH,
        )

    def z_copy(b, step):
        part = pl.ds(pl.multiple_of(chip * piece, 8), piece)
        return pltpu.make_async_remote_copy(
            src_ref=panel.at[b, part], dst_ref=panel.at[b, part],
            send_sem=z_send.at[b, step], recv_sem=z_recv.at[b],
            device_id=(along_z(step), grid), device_id_type=MESH,
        )

    def y_copy(b, step):
        part = pl.ds(pl.multiple_of(yy * share, 8), share)
        return pltpu.make_async_remote_copy(
            src_ref=panel.at[b, part], dst_ref=panel.at[b, part],
            send_sem=y_send.at[b, step], recv_sem=y_recv.at[b],
            device_id=(along_y(step), grid), device_id_type=MESH,
        )

    def sibling_copy(b):
        return pltpu.make_async_remote_copy(
            src_ref=panel.at[b], dst_ref=panel.at[b],
            send_sem=sib_send.at[b], recv_sem=sib_recv.at[b],
            device_id=(sibling, grid), device_id_type=MESH,
        )

    def self_copy(b):
        return pltpu.make_async_copy(filt.at[b], panel.at[b], copy_sem.at[b])

    def phase_scatter(b):
        @pl.when(root)
        def _():
            @pl.loop(1, chips)
            def _(to):
                scatter_copy(b, to).start()

            self_copy(b).start()

    def phase_z(b):
        @pl.when(root)
        def _():
            self_copy(b).wait()

        @pl.when(follower)
        def _():
            scatter_copy(b, chip).wait_recv()

        @pl.when(main)
        def _():
            for step in range(1, n_zh):
                @pl.when(along_z(step) != 0)
                def _():
                    z_copy(b, step).start()

    def phase_y(b):
        if n_zh > 1:
            @pl.when(follower)
            def _():
                most = panel.at[b, pl.ds(0, share - piece)]
                pltpu.make_async_copy(most, most, z_recv.at[b]).wait()

        @pl.when(main)
        def _():
            for step in range(1, n_y):
                @pl.when(along_y(step) != 0)
                def _():
                    y_copy(b, step).start()

    def phase_sibling(b):
        if n_y > 1:
            @pl.when(follower)
            def _():
                most = panel.at[b, pl.ds(0, plane_rows - share)]
                pltpu.make_async_copy(most, most, y_recv.at[b]).wait()

        @pl.when(main)
        def _():
            sibling_copy(b).start()

    def phase_last(b):
        @pl.when(core == 1)
        def _():
            sibling_copy(b).wait_recv()

    @pl.loop(0, norb)
    def _(b):
        inner_terms(ext2, b, 1)
        wait_halos(b, 1, False)

        def store(x, first, place, total):
            before = ext1[b, pl.ds(pl.multiple_of(reach_rows + x * ny + first, 8), 8), :]
            filt[b, place, :] = 2.0 * total - before

        along_x(ext2, b, store)
        phase_scatter(b)

        @pl.when(b >= 1)
        def _():
            phase_z(b - 1)

        @pl.when(b >= 2)
        def _():
            phase_y(b - 2)

        @pl.when(b >= 3)
        def _():
            phase_sibling(b - 3)

    phase_z(norb - 1)
    phase_y(norb - 2)
    phase_sibling(norb - 3)
    phase_y(norb - 1)
    phase_sibling(norb - 2)
    phase_sibling(norb - 1)
    for b in range(norb):
        phase_last(b)

    couples = [(k, m) for k in range(norb) for m in range(k + 1)]
    n_pairs = len(couples) + norb * norb

    def add_pairs(t, sums):
        place = pl.ds(pl.multiple_of(t * 8, 8), 8)
        p = [panel[k, place, :] for k in range(norb)]
        f = [filt[n, place, :] for n in range(norb)]
        terms = [p[k] * p[m] for k, m in couples] + [p[k] * f[n] for k in range(norb) for n in range(norb)]
        return tuple(s + term for s, term in zip(sums, terms))

    sums = lax.fori_loop(
        0, plane_rows // 8, add_pairs, tuple(jnp.zeros((8, LANES), f32) for _ in range(n_pairs))
    )
    pairs[...] = jnp.zeros(pairs.shape, f32)
    for i, s in enumerate(sums):
        pairs[i : i + 1, :] = jnp.sum(s, axis=0, keepdims=True)
    gram_out[...] = jnp.sum(pairs[...].T.reshape(LANES // 8, 8, LANES), axis=0)

    def gram_copy(step):
        return pltpu.make_async_remote_copy(
            src_ref=gram_out, dst_ref=gram_in.at[step],
            send_sem=gram_send.at[step], recv_sem=gram_recv.at[step],
            device_id=(band, peer(step)), device_id_type=MESH,
        )

    for step in range(1, n_grid):
        gram_copy(step).start()
    total = gram_out[...]
    for step in range(1, n_grid):
        gram_copy(step).wait_recv()
        total = total + gram_in[step]
    total = jnp.sum(total, axis=0, keepdims=True) * (1.0 / (plane_rows * LANES * n_grid))
    lane1 = lax.broadcasted_iota(jnp.int32, (1, LANES), 1)

    def number(i):
        one = jnp.sum(jnp.where(lane1 == i, total, 0.0), axis=1, keepdims=True)
        return jnp.broadcast_to(one, (8, LANES))

    gram = {couple: number(i) for i, couple in enumerate(couples)}
    raw = [[number(len(couples) + k * norb + n) for n in range(norb)] for k in range(norb)]
    lower, inverse = {}, {}
    for j in range(norb):
        left = gram[j, j]
        for m in range(j):
            left = left - lower[j, m] * lower[j, m]
        lower[j, j] = jnp.sqrt(left)
        inverse[j, j] = 1.0 / lower[j, j]
        for i in range(j + 1, norb):
            left = gram[i, j]
            for m in range(j):
                left = left - lower[i, m] * lower[j, m]
            lower[i, j] = left * inverse[j, j]
    for j in range(norb):
        for i in range(j + 1, norb):
            left = lower[i, j] * inverse[j, j]
            for m in range(j + 1, i):
                left = left + lower[i, m] * inverse[m, j]
            inverse[i, j] = -left * inverse[i, i]
    corr = [
        [sum(inverse[k, m] * raw[m][n] for m in range(k + 1)) for n in range(norb)]
        for k in range(norb)
    ]
    weight = [[None] * norb for _ in range(norb)]
    zero8 = jnp.zeros((8, LANES), f32)
    for m in range(norb):
        for n in range(norb):
            away = -sum(inverse[k, m] * corr[k][n] for k in range(m, norb))
            weight[m][n] = jnp.where(root, inverse[n, m] if m <= n else zero8, away)
    keep = jnp.where(root, zero8, jnp.ones((8, LANES), f32))

    @pl.loop(0, plane_rows // 8)
    def _(t):
        place = pl.ds(pl.multiple_of(t * 8, 8), 8)
        p = [panel[k, place, :] for k in range(norb)]
        for n in range(norb):
            value = keep * filt[n, place, :]
            for m in range(norb):
                value = value + weight[m][n] * p[m]
            out_ref[n, place, :] = value

    @pl.loop(0, norb)
    def _(b):
        wait_halos(b, 0, True)
        wait_halos(b, 1, True)
        for app in range(2):
            for d in range(len(COEF_STEPS)):
                coef_copy(app, b, d).wait_send()

        @pl.when(root)
        def _():
            @pl.loop(1, chips)
            def _(to):
                scatter_copy(b, to).wait_send()

        @pl.when(main)
        def _():
            for step in range(1, n_zh):
                @pl.when(along_z(step) != 0)
                def _():
                    z_copy(b, step).wait_send()

            for step in range(1, n_y):
                @pl.when(along_y(step) != 0)
                def _():
                    y_copy(b, step).wait_send()

            sibling_copy(b).wait_send()

    for k in range(2):
        coup_copy(k).wait_send()
    for step in range(1, n_grid):
        gram_copy(step).wait_send()


def local(n_band, n_grid, orbitals, potential, projectors, coupling, entry_cell, entry_atom):
    norb, nx, ny, nz = orbitals.shape
    ent = entry_cell.shape[0]
    rows = nx * ny
    chips = n_band // 2
    f32, bf16 = jnp.float32, jnp.bfloat16
    vmem, dma = pltpu.VMEM, pltpu.SemaphoreType.DMA
    ext_rows = rows + 2 * REACH * ny
    whole = pl.BlockSpec(memory_space=pltpu.VMEM)
    out = pl.pallas_call(
        functools.partial(kernel, n_band, n_grid, nx, ny, ent),
        out_shape=jax.ShapeDtypeStruct((norb, rows, nz), f32),
        in_specs=[pl.BlockSpec(memory_space=pltpu.HBM)] * 6,
        out_specs=whole,
        scratch_shapes=[
            vmem((rows, nz), f32),
            vmem(projectors.shape, f32),
            vmem((4, 4, ATOM_DEV), f32),
            vmem((1, ent), jnp.int32),
            vmem((1, ent), jnp.int32),
            vmem((norb, ext_rows, nz), f32),
            vmem((norb, ext_rows, nz), f32),
            vmem((norb, rows, nz), f32),
            vmem((norb, rows, nz), f32),
            vmem((ent, rows), bf16),
            vmem((rows, ent), bf16),
            vmem((ent, LANES), bf16),
            vmem((2 * LANES, ent), bf16),
            vmem((ent, 2 * LANES), bf16),
            vmem((ent, 2 * LANES), bf16),
            vmem((ent, 2 * LANES), bf16),
            vmem((norb, rows, 2 * LANES), bf16),
            vmem((rows, LANES), f32),
            vmem((2 * LANES, 2 * LANES), bf16),
            vmem((2 * LANES, 2 * LANES), bf16),
            vmem((ent, 8), f32),
            vmem((2, norb, 8, LANES), f32),
            vmem((2, norb, 4, 8, LANES), f32),
            vmem((8, LANES), f32),
            vmem((2, 8, LANES), f32),
            vmem((32, LANES), f32),
            vmem((LANES, LANES), f32),
            vmem((8, LANES), f32),
            vmem((n_grid, 8, LANES), f32),
            dma((5,)),
            dma((norb,)),
            dma((2, norb, 2)), dma((2, norb, 2)),
            dma((2, norb, 4)), dma((2, norb, 4)),
            dma((2,)), dma((2,)),
            dma((norb, chips)), dma((norb,)),
            dma((norb, 4)), dma((norb,)),
            dma((norb, 16)), dma((norb,)),
            dma((norb,)), dma((norb,)),
            dma((norb,)),
            dma((n_grid,)), dma((n_grid,)),
        ],
        compiler_params=pltpu.CompilerParams(
            collective_id=0, has_side_effects=True, vmem_limit_bytes=62 * 1024 * 1024
        ),
        name="filter_panel",
    )(
        orbitals.reshape(norb, rows, nz),
        potential.reshape(rows, nz),
        projectors,
        coupling.transpose(1, 2, 0),
        entry_cell.reshape(1, ent),
        entry_atom.reshape(1, ent),
    )
    return out.reshape(orbitals.shape)


def solution(mesh):
    return jax.shard_map(
        functools.partial(local, mesh.shape["band"], mesh.shape["grid"]),
        mesh=mesh,
        in_specs=(
            P("band", "grid", None, None),
            P("grid", None, None),
            P(None, "grid"),
            P("grid", None, None),
            P("grid"),
            P("grid"),
        ),
        out_specs=P("band", "grid", None, None),
        check_vma=False,
    )
```

```python
import functools
import math

import jax
import jax.numpy as jnp
from jax import lax
from jax.experimental import pallas as pl
from jax.experimental.pallas import tpu as pltpu
from jax.sharding import PartitionSpec as P

CENTER = 34.0
HALF = 30.0
SPACING = 0.5
REACH = 6
LANES = 128
ATOM_DEV = 8
GROUP = 32
TILE = 256
LAG = 1
TURN = 2
WIDE = 512
MESH = pl.DeviceIdType.MESH
COEF_STEPS = (-2, -1, 1, 2)


def stencil_weights():
    fact = math.factorial
    side = [
        2.0 * (-1.0) ** (k + 1) * fact(REACH) ** 2 / (k * k * fact(REACH - k) * fact(REACH + k))
        for k in range(1, REACH + 1)
    ]
    return -2.0 * sum(side), side


C0, CK = stencil_weights()
KIN = -0.5 / (SPACING * SPACING)
DIAG = (3.0 * KIN * C0 - CENTER) / HALF
EK = [KIN * c / HALF for c in CK]


def split(x):
    high = x.astype(jnp.bfloat16)
    return high, (x - high.astype(jnp.float32)).astype(jnp.bfloat16)


def dot(a, b):
    return jnp.dot(a, b, preferred_element_type=jnp.float32)


def kernel(
    n_band, n_grid, nx, ny, ent,
    orb_ref, pot_hbm, proj_hbm, coup_hbm, cell_hbm, atom_hbm,
    out_ref,
    pot_ref, proj_ref, coup_ref, cell_ref, atom_ref,
    ext1, ext2, filt, panel, rows_m, rows_t, lane_m, m_row, m_col, picked, spread, vcat, acc,
    zmat, wcat, cols, coef_out, coef_in, coup_own, coup_in, mix, pairs, gram_out, gram_in,
    load_sem, turn_sem, own_sem, halo_send, halo_recv, coef_send, coef_recv, coup_send, coup_recv,
    scat_send, scat_recv, z_send, z_recv, y_send, y_recv, sib_send, sib_recv, copy_sem,
    gram_send, gram_recv,
):
    f32, bf16 = jnp.float32, jnp.bfloat16
    norb = orb_ref.shape[0]
    plane_rows = nx * ny
    reach_rows = REACH * ny
    chips = n_band // 2
    n_zh = 4 if chips % 4 == 0 else 1
    n_y = chips // n_zh
    ringed = n_zh > 1
    share = plane_rows // n_y
    half = share // 2
    band, grid = lax.axis_index("band"), lax.axis_index("grid")
    chip = lax.div(band, 2)
    zh, yy = lax.rem(chip, n_zh), lax.div(chip, n_zh)
    core = lax.rem(band, 2)
    sibling = band + 1 - 2 * core
    main = core == 0
    has_left, has_right = grid > 0, grid < n_grid - 1

    def peer(step):
        return lax.rem(grid + step + n_grid, n_grid)

    loads = [
        pltpu.make_async_copy(source, there, load_sem.at[i])
        for i, (source, there) in enumerate(
            [
                (cell_hbm, cell_ref), (atom_hbm, atom_ref), (proj_hbm, proj_ref),
                (coup_hbm, coup_ref), (pot_hbm, pot_ref),
            ]
        )
    ]
    for load in loads:
        load.start()

    barrier = pltpu.get_barrier_semaphore()
    for step in range(1, n_grid):
        pl.semaphore_signal(barrier, inc=1, device_id=(band, peer(step)), device_id_type=MESH)
    pl.semaphore_signal(barrier, inc=1, device_id=(sibling, grid), device_id_type=MESH)

    def along_z(step):
        return 2 * (yy * n_zh + lax.rem(zh + step, n_zh))

    def along_y(step):
        return 2 * (lax.rem(yy + step, n_y) * n_zh + zh)

    root = band == 0
    follower = main & jnp.logical_not(root)
    greeted = [along_z(step) for step in (1, n_zh - 1)] if ringed else []
    greeted += [along_y(step) for step in range(1, n_y)]

    @pl.when(main)
    def _():
        for to in greeted:
            pl.semaphore_signal(barrier, inc=1, device_id=(to, grid), device_id_type=MESH)

    @pl.when(follower)
    def _():
        pl.semaphore_wait(barrier, n_grid + len(greeted))

    @pl.when(core == 1)
    def _():
        pl.semaphore_wait(barrier, n_grid)

    def halo(source, start, ext, b, app, side):
        step = -1 if side == 0 else 1
        first = start if side == 0 else start + plane_rows - reach_rows
        land = reach_rows + plane_rows if side == 0 else 0
        return pltpu.make_async_remote_copy(
            src_ref=source.at[b, pl.ds(first, reach_rows)],
            dst_ref=ext.at[b, pl.ds(land, reach_rows)],
            send_sem=halo_send.at[app, b, side],
            recv_sem=halo_recv.at[app, b, 1 - side],
            device_id=(band, grid + step),
            device_id_type=MESH,
        )

    def halo_source(app):
        return (orb_ref, 0, ext1) if app == 0 else (ext2, reach_rows, ext2)

    def send_halos(b, app):
        source, start, ext = halo_source(app)

        @pl.when(has_left)
        def _():
            halo(source, start, ext, b, app, 0).start()

        @pl.when(has_right)
        def _():
            halo(source, start, ext, b, app, 1).start()

    def wait_halos(b, app, sent):
        source, start, ext = halo_source(app)

        @pl.when(has_left)
        def _():
            if sent:
                halo(source, start, ext, b, app, 0).wait_send()
            else:
                halo(source, start, ext, b, app, 1).wait_recv()

        @pl.when(has_right)
        def _():
            if sent:
                halo(source, start, ext, b, app, 1).wait_send()
            else:
                halo(source, start, ext, b, app, 0).wait_recv()

    def own_copy(b):
        return pltpu.make_async_copy(
            orb_ref.at[b], ext1.at[b, pl.ds(reach_rows, plane_rows)], own_sem.at[b]
        )

    waits_turn = band == 1

    @pl.loop(0, norb)
    def _(b):
        own_copy(b).start()

        @pl.when(band > 1)
        def _():
            send_halos(b, 0)

    for load in loads[:4]:
        load.wait()
    coup_own[...] = jnp.zeros(coup_own.shape, f32)
    for i in range(4):
        first = GROUP * i + ATOM_DEV
        coup_own[0:4, first : first + ATOM_DEV] = coup_ref[i]

    def coup_copy(k):
        return pltpu.make_async_remote_copy(
            src_ref=coup_own, dst_ref=coup_in.at[k],
            send_sem=coup_send.at[k], recv_sem=coup_recv.at[k],
            device_id=(band, peer((-1, 1)[k])), device_id_type=MESH,
        )

    zero_halo = jnp.zeros((norb, reach_rows, LANES), f32)
    for ext in (ext1, ext2):
        @pl.when(jnp.logical_not(has_left))
        def _():
            ext[:, 0:reach_rows] = zero_halo

        @pl.when(jnp.logical_not(has_right))
        def _():
            ext[:, reach_rows + plane_rows :] = zero_halo

    cell = cell_ref[...]
    atom = atom_ref[...]
    row_of = lax.shift_right_logical(cell, 7)
    lane_of = jnp.bitwise_and(cell, LANES - 1)
    near = jnp.where(atom >= 0, atom - (grid - 1) * ATOM_DEV, -1000)
    for j in range(4):
        hit = lax.broadcasted_iota(jnp.int32, (GROUP, ent), 0) == near
        high, low = split(jnp.where(hit, proj_ref[j : j + 1, :], 0.0))
        m_row[GROUP * j : GROUP * (j + 1)] = high
        m_row[LANES + GROUP * j : LANES + GROUP * (j + 1)] = low
    packed = jnp.concatenate(
        [row_of.astype(f32), lane_of.astype(f32), near.astype(f32), near.astype(f32), proj_ref[...]],
        axis=0,
    )
    cols[...] = packed.T

    @pl.loop(0, ent // TILE)
    def _(i):
        part = pl.ds(pl.multiple_of(i * TILE, TILE), TILE)
        column = cols[part, :]
        lane = lax.broadcasted_iota(jnp.int32, (TILE, LANES), 1).astype(f32)
        wide = lax.broadcasted_iota(jnp.int32, (TILE, plane_rows), 1).astype(f32)
        rows_m[part, :] = jnp.where(column[:, 0:1] == wide, 1.0, 0.0).astype(bf16)
        lane_m[part, :] = jnp.where(column[:, 1:2] == lane, 1.0, 0.0).astype(bf16)

    @pl.when(root)
    def _():
        pl.semaphore_wait(barrier, n_grid + len(greeted))

        @pl.loop(0, norb)
        def _(b):
            send_halos(b, 0)

    for k in range(2):
        coup_copy(k).start()

    apart = jnp.abs(
        lax.broadcasted_iota(jnp.int32, (LANES, LANES), 0)
        - lax.broadcasted_iota(jnp.int32, (LANES, LANES), 1)
    )
    band_m = jnp.zeros((LANES, LANES), f32)
    for k in range(1, REACH + 1):
        band_m = jnp.where(apart == k, EK[k - 1], band_m)
    high, low = split(band_m)
    zmat[0:LANES, 0:LANES] = high
    zmat[0:LANES, LANES:] = low
    zmat[LANES:, 0:LANES] = high
    zmat[LANES:, LANES:] = jnp.zeros((LANES, LANES), bf16)

    def coef_copy(app, b, d):
        return pltpu.make_async_remote_copy(
            src_ref=coef_out.at[app, b], dst_ref=coef_in.at[app, b, d],
            send_sem=coef_send.at[app, b, d], recv_sem=coef_recv.at[app, b, d],
            device_id=(band, peer(COEF_STEPS[d])), device_id_type=MESH,
        )

    def cut(ext, b):
        for x in range(nx):
            high, low = split(ext[b, reach_rows + x * ny : reach_rows + (x + 1) * ny, :])
            vcat[b, x * ny : (x + 1) * ny, 0:LANES] = high
            vcat[b, x * ny : (x + 1) * ny, LANES:] = low

    def coefficients(ext, b, app):
        cut(ext, b)

        row = lax.broadcasted_iota(jnp.int32, (ny, LANES), 0)
        steps = ent // WIDE
        for i in range(steps):
            part = slice(i * WIDE, (i + 1) * WIDE)
            got = dot(rows_m[part, :], vcat[b]).astype(bf16)
            mask = lane_m[part, :]
            picked[part, 0:LANES] = got[:, 0:LANES] * mask
            picked[part, LANES:] = got[:, LANES:] * mask
            for x in range(i * nx // steps, (i + 1) * nx // steps):
                place = slice(x * ny, (x + 1) * ny)
                cells = ext[b, reach_rows + x * ny : reach_rows + (x + 1) * ny, :]
                both = dot(vcat[b, place, :], zmat[...])
                total = both[:, 0:LANES] + both[:, LANES:]
                for k in range(1, REACH + 1):
                    before = jnp.where(row >= k, pltpu.roll(cells, k, 0), 0.0)
                    after = jnp.where(row < ny - k, pltpu.roll(cells, ny - k, 0), 0.0)
                    total = total + EK[k - 1] * (before + after)
                acc[b, place, :] = total

        both = dot(m_row[...], picked[...])
        both = both[0:LANES] + both[LANES:]
        both = (both[:, 0:LANES] + both[:, LANES:]).T
        coef_out[app, b] = jnp.sum(both.reshape(LANES // 8, 8, LANES), axis=0)
        for d in range(len(COEF_STEPS)):
            coef_copy(app, b, d).start()

    lane8 = lax.broadcasted_iota(jnp.int32, (8, LANES), 1)
    slot8 = jnp.bitwise_and(lax.shift_right_logical(lane8, 3), 3)

    def near_total(app, b):
        total = coef_out[app, b]
        for d, step in enumerate(COEF_STEPS):
            coef_copy(app, b, d).wait_recv()
            shift = -step
            there = grid + shift
            lands = slot8 + shift
            keep = (slot8 < 3) & (lands >= 0) & (lands < 3) & (there >= 0) & (there < n_grid)
            total = total + pltpu.roll(
                jnp.where(keep, coef_in[app, b, d], 0.0), (8 * shift) % LANES, 1
            )
        return jnp.broadcast_to(jnp.sum(total, axis=0, keepdims=True), (8, LANES))

    def coupling_rows():
        total = coup_own[...]
        for k, step in enumerate((-1, 1)):
            coup_copy(k).wait_recv()
            shift = -step
            there = grid + shift
            keep = (there >= 0) & (there < n_grid)
            total = total + pltpu.roll(
                jnp.where(keep, coup_in[k], 0.0), (8 * shift) % LANES, 1
            )
        group = lax.shift_right_logical(lax.broadcasted_iota(jnp.int32, (1, LANES), 1), 5)
        for k in range(4):
            line = jnp.zeros((1, LANES), f32)
            for i in range(4):
                j = (i + k) % 4
                line = jnp.where(group == i, total[j : j + 1], line)
            mix[8 * k : 8 * k + 8, :] = jnp.broadcast_to(line * (1.0 / HALF), (8, LANES))

    def inner_terms(ext, b, app):
        near_c = near_total(app, b)
        mixed = mix[0:8, :] * near_c
        for k in range(1, 4):
            mixed = mixed + mix[8 * k : 8 * k + 8, :] * pltpu.roll(near_c, LANES - GROUP * k, 1)
        high, low = split(jnp.broadcast_to(mixed[0:1], (LANES, LANES)).T)
        wcat[0:LANES, 0:LANES] = high
        wcat[0:LANES, LANES:] = low
        wcat[LANES:, 0:LANES] = high
        wcat[LANES:, LANES:] = jnp.zeros((LANES, LANES), bf16)

        for i in range(0, ent, WIDE):
            back = dot(m_col[i : i + WIDE, :], wcat[...])
            high, low = split(back[:, 0:LANES] + back[:, LANES:])
            mask = lane_m[i : i + WIDE, :]
            spread[i : i + WIDE, 0:LANES] = high * mask
            spread[i : i + WIDE, LANES:] = low * mask

        step = 4 * ny

        for i in range(0, plane_rows, step):
            both = dot(rows_t[i : i + step, :], spread[...])
            acc[b, i : i + step, :] = acc[b, i : i + step, :] + (both[:, 0:LANES] + both[:, LANES:])

    def along_x(ext, b, store):
        @pl.loop(0, ny // 8)
        def _(t):
            first = pl.multiple_of(t * 8, 8)
            cells = [
                ext[b, pl.ds(pl.multiple_of(x * ny + first, 8), 8), :]
                for x in range(nx + 2 * REACH)
            ]
            for x in range(nx):
                place = pl.ds(pl.multiple_of(x * ny + first, 8), 8)
                here = cells[x + REACH]
                total = acc[b, place, :] + here * (pot_ref[place, :] * (1.0 / HALF) + DIAG)
                for k in range(1, REACH + 1):
                    total = total + EK[k - 1] * (cells[x + REACH + k] + cells[x + REACH - k])
                store(x, first, place, total)

    @pl.loop(0, norb)
    def _(b):
        own_copy(b).wait()
        coefficients(ext1, b, 0)

    @pl.when(waits_turn)
    def _():
        pl.semaphore_wait(turn_sem, 1)

        @pl.loop(0, norb)
        def _(b):
            send_halos(b, 0)

    @pl.loop(0, ent // TILE)
    def _(i):
        part = pl.ds(pl.multiple_of(i * TILE, TILE), TILE)
        column = cols[part, :]
        lane = lax.broadcasted_iota(jnp.int32, (TILE, LANES), 1).astype(f32)
        total = jnp.zeros((TILE, LANES), f32)
        for j in range(4):
            total = jnp.where(column[:, 2:3] + (GROUP * j) == lane, column[:, 4 + j : 5 + j], total)
        high, low = split(total)
        m_col[part, 0:LANES] = high
        m_col[part, LANES:] = low

    @pl.loop(0, nx)
    def _(x):
        first = pl.multiple_of(x * ny, ny)
        down = lax.broadcasted_iota(jnp.int32, (ny, ent), 0) + first
        rows_t[pl.ds(first, ny), :] = jnp.where(down == row_of, 1.0, 0.0).astype(bf16)

    coupling_rows()
    loads[4].wait()

    @pl.loop(0, norb)
    def _(b):
        inner_terms(ext1, b, 0)
        wait_halos(b, 0, False)

        def store(x, first, place, total):
            ext2[b, pl.ds(pl.multiple_of(reach_rows + x * ny + first, 8), 8), :] = total

        along_x(ext1, b, store)
        send_halos(b, 1)

        @pl.when(root & (b == TURN))
        def _():
            pl.semaphore_signal(turn_sem, inc=1, device_id=(1, grid), device_id_type=MESH)

        coefficients(ext2, b, 1)

    def share_of(y):
        return pl.ds(pl.multiple_of(y * share, 8), share)

    def scatter_copy(b, y):
        return pltpu.make_async_remote_copy(
            src_ref=filt.at[b, share_of(y)], dst_ref=panel.at[b, share_of(y)],
            send_sem=scat_send.at[b, y], recv_sem=scat_recv.at[b],
            device_id=(2 * n_zh * y, grid), device_id_type=MESH,
        )

    def z_copy(source, b, way):
        part = pl.ds(pl.multiple_of(yy * share, 8), share)
        return pltpu.make_async_remote_copy(
            src_ref=source.at[b, part], dst_ref=panel.at[b, part],
            send_sem=z_send.at[b, way], recv_sem=z_recv.at[b, way],
            device_id=(along_z(n_zh - 1 if way else 1), grid), device_id_type=MESH,
        )

    def z_relay(b, way):
        part = pl.ds(pl.multiple_of(yy * share + way * half, 8), half)
        return pltpu.make_async_remote_copy(
            src_ref=panel.at[b, part], dst_ref=panel.at[b, part],
            send_sem=z_send.at[b, way], recv_sem=z_recv.at[b, way],
            device_id=(along_z(n_zh - 1 if way else 1), grid), device_id_type=MESH,
        )

    def y_copy(source, b, step):
        return pltpu.make_async_remote_copy(
            src_ref=source.at[b, share_of(yy)], dst_ref=panel.at[b, share_of(yy)],
            send_sem=y_send.at[b, step], recv_sem=y_recv.at[b],
            device_id=(along_y(step), grid), device_id_type=MESH,
        )

    def y_copies(source, b, act):
        for step in range(1, n_y):
            @pl.when(along_y(step) != 0)
            def _():
                act(y_copy(source, b, step))

    def sibling_copy(source, b):
        return pltpu.make_async_remote_copy(
            src_ref=source.at[b], dst_ref=panel.at[b],
            send_sem=sib_send.at[b], recv_sem=sib_recv.at[b],
            device_id=(sibling, grid), device_id_type=MESH,
        )

    def self_copy(b):
        return pltpu.make_async_copy(filt.at[b], panel.at[b], copy_sem.at[b])

    def start(copy):
        copy.start()

    def root_sends(b):
        @pl.when(root)
        def _():
            for y in range(1, n_y):
                scatter_copy(b, y).start()
            if ringed:
                for way in range(2):
                    z_copy(filt, b, way).start()
            y_copies(filt, b, start)
            sibling_copy(filt, b).start()
            self_copy(b).start()

    def at(z):
        return follower & (zh == z)

    def phase(k, b):
        if k == 0:
            @pl.when(at(0))
            def _():
                scatter_copy(b, yy).wait_recv()
                if ringed:
                    for way in range(2):
                        z_copy(panel, b, way).start()
                y_copies(panel, b, start)

        if k == 1 and ringed:
            for z, way in ((1, 0), (3, 1)):
                @pl.when(at(z))
                def _():
                    z_copy(panel, b, way).wait_recv()
                    z_relay(b, way).start()
                    y_copies(panel, b, start)

        if k == 2 and ringed:
            @pl.when(at(2))
            def _():
                for way in range(2):
                    z_relay(b, way).wait_recv()
                y_copies(panel, b, start)

        if k == 3:
            @pl.when(follower)
            def _():
                if n_y > 1:
                    most = panel.at[b, pl.ds(0, plane_rows - share)]
                    pltpu.make_async_copy(most, most, y_recv.at[b]).wait()
                sibling_copy(panel, b).start()

    def slot(t):
        for k in range(4):
            b = t - k
            if isinstance(t, int):
                if 0 <= b < norb:
                    phase(k, b)
                continue

            @pl.when((b >= 0) & (b < norb))
            def _():
                phase(k, b)

    def phase_last(b):
        @pl.when(core == 1)
        def _():
            sibling_copy(panel, b).wait_recv()

    @pl.loop(0, norb)
    def _(b):
        inner_terms(ext2, b, 1)
        slot(2 * b - LAG)
        wait_halos(b, 1, False)

        def store(x, first, place, total):
            before = ext1[b, pl.ds(pl.multiple_of(reach_rows + x * ny + first, 8), 8), :]
            filt[b, place, :] = 2.0 * total - before

        along_x(ext2, b, store)
        root_sends(b)
        slot(2 * b + 1 - LAG)

    for t in range(2 * norb - LAG, norb + 3):
        slot(t)

    @pl.when(root)
    def _():
        for b in range(norb):
            self_copy(b).wait()

    for b in range(norb):
        phase_last(b)

    couples = [(k, m) for k in range(norb) for m in range(k + 1)]
    n_pairs = len(couples) + norb * norb

    def add_pairs(t, sums):
        place = pl.ds(pl.multiple_of(t * 8, 8), 8)
        p = [panel[k, place, :] for k in range(norb)]
        f = [filt[n, place, :] for n in range(norb)]
        terms = [p[k] * p[m] for k, m in couples] + [p[k] * f[n] for k in range(norb) for n in range(norb)]
        return tuple(s + term for s, term in zip(sums, terms))

    sums = lax.fori_loop(
        0, plane_rows // 8, add_pairs, tuple(jnp.zeros((8, LANES), f32) for _ in range(n_pairs))
    )
    pairs[...] = jnp.zeros(pairs.shape, f32)
    for i, s in enumerate(sums):
        pairs[i : i + 1, :] = jnp.sum(s, axis=0, keepdims=True)
    gram_out[...] = jnp.sum(pairs[...].T.reshape(LANES // 8, 8, LANES), axis=0)

    def gram_copy(step):
        return pltpu.make_async_remote_copy(
            src_ref=gram_out, dst_ref=gram_in.at[step],
            send_sem=gram_send.at[step], recv_sem=gram_recv.at[step],
            device_id=(band, peer(step)), device_id_type=MESH,
        )

    for step in range(1, n_grid):
        gram_copy(step).start()
    total = gram_out[...]
    for step in range(1, n_grid):
        gram_copy(step).wait_recv()
        total = total + gram_in[step]
    total = jnp.sum(total, axis=0, keepdims=True) * (1.0 / (plane_rows * LANES * n_grid))
    lane1 = lax.broadcasted_iota(jnp.int32, (1, LANES), 1)

    def number(i):
        one = jnp.sum(jnp.where(lane1 == i, total, 0.0), axis=1, keepdims=True)
        return jnp.broadcast_to(one, (8, LANES))

    gram = {couple: number(i) for i, couple in enumerate(couples)}
    raw = [[number(len(couples) + k * norb + n) for n in range(norb)] for k in range(norb)]
    lower, inverse = {}, {}
    for j in range(norb):
        left = gram[j, j]
        for m in range(j):
            left = left - lower[j, m] * lower[j, m]
        lower[j, j] = jnp.sqrt(left)
        inverse[j, j] = 1.0 / lower[j, j]
        for i in range(j + 1, norb):
            left = gram[i, j]
            for m in range(j):
                left = left - lower[i, m] * lower[j, m]
            lower[i, j] = left * inverse[j, j]
    for j in range(norb):
        for i in range(j + 1, norb):
            left = lower[i, j] * inverse[j, j]
            for m in range(j + 1, i):
                left = left + lower[i, m] * inverse[m, j]
            inverse[i, j] = -left * inverse[i, i]
    corr = [
        [sum(inverse[k, m] * raw[m][n] for m in range(k + 1)) for n in range(norb)]
        for k in range(norb)
    ]
    weight = [[None] * norb for _ in range(norb)]
    zero8 = jnp.zeros((8, LANES), f32)
    for m in range(norb):
        for n in range(norb):
            away = -sum(inverse[k, m] * corr[k][n] for k in range(m, norb))
            weight[m][n] = jnp.where(root, inverse[n, m] if m <= n else zero8, away)
    keep = jnp.where(root, zero8, jnp.ones((8, LANES), f32))

    @pl.loop(0, plane_rows // 8)
    def _(t):
        place = pl.ds(pl.multiple_of(t * 8, 8), 8)
        p = [panel[k, place, :] for k in range(norb)]
        for n in range(norb):
            value = keep * filt[n, place, :]
            for m in range(norb):
                value = value + weight[m][n] * p[m]
            out_ref[n, place, :] = value

    @pl.loop(0, norb)
    def _(b):
        wait_halos(b, 0, True)
        wait_halos(b, 1, True)
        for app in range(2):
            for d in range(len(COEF_STEPS)):
                coef_copy(app, b, d).wait_send()

        def ended(copy):
            copy.wait_send()

        @pl.when(root)
        def _():
            for y in range(1, n_y):
                scatter_copy(b, y).wait_send()

        @pl.when(main)
        def _():
            if ringed:
                for way in range(2):
                    @pl.when(zh == 0)
                    def _():
                        z_copy(panel, b, way).wait_send()

                    @pl.when(zh == (1, 3)[way])
                    def _():
                        z_relay(b, way).wait_send()

            y_copies(panel, b, ended)
            sibling_copy(panel, b).wait_send()

    for k in range(2):
        coup_copy(k).wait_send()
    for step in range(1, n_grid):
        gram_copy(step).wait_send()


def local(n_band, n_grid, orbitals, potential, projectors, coupling, entry_cell, entry_atom):
    norb, nx, ny, nz = orbitals.shape
    ent = entry_cell.shape[0]
    rows = nx * ny
    chips = n_band // 2
    f32, bf16 = jnp.float32, jnp.bfloat16
    vmem, dma = pltpu.VMEM, pltpu.SemaphoreType.DMA
    ext_rows = rows + 2 * REACH * ny
    whole = pl.BlockSpec(memory_space=pltpu.VMEM)
    out = pl.pallas_call(
        functools.partial(kernel, n_band, n_grid, nx, ny, ent),
        out_shape=jax.ShapeDtypeStruct((norb, rows, nz), f32),
        in_specs=[pl.BlockSpec(memory_space=pltpu.HBM)] * 6,
        out_specs=whole,
        scratch_shapes=[
            vmem((rows, nz), f32),
            vmem(projectors.shape, f32),
            vmem((4, 4, ATOM_DEV), f32),
            vmem((1, ent), jnp.int32),
            vmem((1, ent), jnp.int32),
            vmem((norb, ext_rows, nz), f32),
            vmem((norb, ext_rows, nz), f32),
            vmem((norb, rows, nz), f32),
            vmem((norb, rows, nz), f32),
            vmem((ent, rows), bf16),
            vmem((rows, ent), bf16),
            vmem((ent, LANES), bf16),
            vmem((2 * LANES, ent), bf16),
            vmem((ent, 2 * LANES), bf16),
            vmem((ent, 2 * LANES), bf16),
            vmem((ent, 2 * LANES), bf16),
            vmem((norb, rows, 2 * LANES), bf16),
            vmem((norb, rows, LANES), f32),
            vmem((2 * LANES, 2 * LANES), bf16),
            vmem((2 * LANES, 2 * LANES), bf16),
            vmem((ent, 8), f32),
            vmem((2, norb, 8, LANES), f32),
            vmem((2, norb, 4, 8, LANES), f32),
            vmem((8, LANES), f32),
            vmem((2, 8, LANES), f32),
            vmem((32, LANES), f32),
            vmem((LANES, LANES), f32),
            vmem((8, LANES), f32),
            vmem((n_grid, 8, LANES), f32),
            dma((5,)),
            pltpu.SemaphoreType.REGULAR,
            dma((norb,)),
            dma((2, norb, 2)), dma((2, norb, 2)),
            dma((2, norb, 4)), dma((2, norb, 4)),
            dma((2,)), dma((2,)),
            dma((norb, 4)), dma((norb,)),
            dma((norb, 2)), dma((norb, 2)),
            dma((norb, 4)), dma((norb,)),
            dma((norb,)), dma((norb,)),
            dma((norb,)),
            dma((n_grid,)), dma((n_grid,)),
        ],
        compiler_params=pltpu.CompilerParams(
            collective_id=0, has_side_effects=True, vmem_limit_bytes=40 * 1024 * 1024
        ),
        name="filter_panel",
    )(
        *[pltpu.with_memory_space_constraint(v, pltpu.HBM) for v in (orbitals.reshape(norb, rows, nz),
        potential.reshape(rows, nz),
        projectors,
        coupling.transpose(1, 2, 0),
        entry_cell.reshape(1, ent),
        entry_atom.reshape(1, ent))]
    )
    return out.reshape(orbitals.shape)


def solution(mesh):
    return jax.shard_map(
        functools.partial(local, mesh.shape["band"], mesh.shape["grid"]),
        mesh=mesh,
        in_specs=(
            P("band", "grid", None, None),
            P("grid", None, None),
            P(None, "grid"),
            P("grid", None, None),
            P("grid"),
            P("grid"),
        ),
        out_specs=P("band", "grid", None, None),
        check_vma=False,
    )
```

```python
import functools
import math

import jax
import jax.numpy as jnp
from jax import lax
from jax.experimental import pallas as pl
from jax.experimental.pallas import tpu as pltpu
from jax.sharding import PartitionSpec as P

CENTER = 34.0
HALF = 30.0
SPACING = 0.5
REACH = 6
LANES = 128
ATOM_DEV = 8
GROUP = 32
TILE = 256
WIDE = 512
MESH = pl.DeviceIdType.MESH
COEF_STEPS = (-2, -1, 1, 2)


def stencil_weights():
    fact = math.factorial
    side = [
        2.0 * (-1.0) ** (k + 1) * fact(REACH) ** 2 / (k * k * fact(REACH - k) * fact(REACH + k))
        for k in range(1, REACH + 1)
    ]
    return -2.0 * sum(side), side


C0, CK = stencil_weights()
KIN = -0.5 / (SPACING * SPACING)
DIAG = (3.0 * KIN * C0 - CENTER) / HALF
EK = [KIN * c / HALF for c in CK]


def split(x):
    high = x.astype(jnp.bfloat16)
    return high, (x - high.astype(jnp.float32)).astype(jnp.bfloat16)


def dot(a, b):
    return jnp.dot(a, b, preferred_element_type=jnp.float32)


def kernel(
    n_band, n_grid, nx, ny, ent,
    orb_ref, pot_hbm, proj_hbm, coup_hbm, cell_hbm, atom_hbm,
    out_ref,
    pot_ref, proj_ref, coup_ref, cell_ref, atom_ref,
    ext1, ext2, fields, rows_m, rows_t, lane_m, m_row, m_col, picked, spread, vcat, acc,
    zmat, wcat, cols, coef_out, coef_in, coup_own, coup_in, mix, pairs, gram_out, gram_in,
    load_sem, own_sem, swap_send, back_send, back_recv, halo_send, halo_recv, coef_send, coef_recv, coup_send, coup_recv,
    scat_send, scat_recv, z_send, z_recv, y_send, y_recv, sib_send, sib_recv,
    gram_send, gram_recv,
):
    f32, bf16 = jnp.float32, jnp.bfloat16
    norb = orb_ref.shape[0]
    plane_rows = nx * ny
    reach_rows = REACH * ny
    chips = n_band // 2
    n_zh = 4 if chips % 4 == 0 else 1
    n_y = chips // n_zh
    ringed = n_zh > 1
    share = plane_rows // n_y
    half = share // 2
    band, grid = lax.axis_index("band"), lax.axis_index("grid")
    chip = lax.div(band, 2)
    zh, yy = lax.rem(chip, n_zh), lax.div(chip, n_zh)
    core = lax.rem(band, 2)
    sibling = band + 1 - 2 * core
    main = core == 0
    paired = band < 2
    filt, panel = fields.at[pl.ds(0, norb)], fields.at[pl.ds(norb, norb)]
    has_left, has_right = grid > 0, grid < n_grid - 1

    def peer(step):
        return lax.rem(grid + step + n_grid, n_grid)

    loads = [
        pltpu.make_async_copy(source, there, load_sem.at[i])
        for i, (source, there) in enumerate(
            [
                (cell_hbm, cell_ref), (atom_hbm, atom_ref), (proj_hbm, proj_ref),
                (coup_hbm, coup_ref), (pot_hbm, pot_ref),
            ]
        )
    ]
    for load in loads:
        load.start()

    barrier = pltpu.get_barrier_semaphore()
    for step in range(1, n_grid):
        pl.semaphore_signal(barrier, inc=1, device_id=(band, peer(step)), device_id_type=MESH)
    pl.semaphore_signal(barrier, inc=1, device_id=(sibling, grid), device_id_type=MESH)

    def along_z(step):
        return 2 * (yy * n_zh + lax.rem(zh + step, n_zh))

    def along_y(step):
        return 2 * (lax.rem(yy + step, n_y) * n_zh + zh)

    root = band == 0
    follower = main & jnp.logical_not(root)
    greeted = [along_z(step) for step in (1, n_zh - 1)] if ringed else []
    greeted += [along_y(step) for step in range(1, n_y)]

    @pl.when(main | paired)
    def _():
        for to in greeted:
            pl.semaphore_signal(barrier, inc=1, device_id=(to, grid), device_id_type=MESH)

    beside_root = follower & ((zh == 0) | ((yy == 0) & (zh != 2)))

    @pl.when(beside_root)
    def _():
        pl.semaphore_signal(barrier, inc=1, device_id=(1, grid), device_id_type=MESH)

    @pl.when(paired)
    def _():
        for step in (-1, 1):
            pl.semaphore_signal(
                barrier, inc=1, device_id=(sibling, peer(step)), device_id_type=MESH
            )

    @pl.when(beside_root)
    def _():
        pl.semaphore_wait(barrier, n_grid + len(greeted) + 1)

    @pl.when(follower & jnp.logical_not(beside_root))
    def _():
        pl.semaphore_wait(barrier, n_grid + len(greeted))

    @pl.when((core == 1) & jnp.logical_not(paired))
    def _():
        pl.semaphore_wait(barrier, n_grid)

    def home(o):
        return jnp.where(paired, o // 2, band), jnp.where(paired, o % 2 + 2 * core, o)

    def halo(b, app, side):
        step = -1 if side == 0 else 1
        start = 0 if app == 0 else reach_rows
        first = start if side == 0 else start + plane_rows - reach_rows
        land = reach_rows + plane_rows if side == 0 else 0
        to_band, place = home(b) if app == 0 else (band, b)
        return pltpu.make_async_remote_copy(
            src_ref=(ext2 if app else orb_ref).at[b, pl.ds(first, reach_rows)],
            dst_ref=(ext2 if app else ext1).at[place, pl.ds(land, reach_rows)],
            send_sem=halo_send.at[app, b, side],
            recv_sem=halo_recv.at[app, place, 1 - side],
            device_id=(to_band, grid + step),
            device_id_type=MESH,
        )

    def arrived(b, app, side):
        ext = ext2 if app else ext1
        land = 0 if side == 0 else reach_rows + plane_rows
        there = ext.at[b, pl.ds(land, reach_rows)]
        return pltpu.make_async_copy(there, there, halo_recv.at[app, b, side])

    def send_halos(b, app):
        @pl.when(has_left)
        def _():
            halo(b, app, 0).start()

        @pl.when(has_right)
        def _():
            halo(b, app, 1).start()

    def wait_halos(b, app, sent):
        @pl.when(has_left)
        def _():
            if sent:
                halo(b, app, 0).wait_send()
            else:
                arrived(b, app, 0).wait()

        @pl.when(has_right)
        def _():
            if sent:
                halo(b, app, 1).wait_send()
            else:
                arrived(b, app, 1).wait()

    def own_copy(b):
        return pltpu.make_async_copy(
            orb_ref.at[b], ext1.at[b, pl.ds(reach_rows, plane_rows)], own_sem.at[b]
        )

    def swap_copy(o):
        place = home(o)[1]
        return pltpu.make_async_remote_copy(
            src_ref=orb_ref.at[o], dst_ref=ext1.at[place, pl.ds(reach_rows, plane_rows)],
            send_sem=swap_send.at[o], recv_sem=own_sem.at[place],
            device_id=(sibling, grid), device_id_type=MESH,
        )

    def stays(o):
        return home(o)[0] == band

    @pl.loop(0, norb)
    def _(o):
        @pl.when(stays(o))
        def _():
            place = home(o)[1]
            pltpu.make_async_copy(
                orb_ref.at[o], ext1.at[place, pl.ds(reach_rows, plane_rows)], own_sem.at[place]
            ).start()

        @pl.when(jnp.logical_not(paired))
        def _():
            send_halos(o, 0)

    for load in loads[:4]:
        load.wait()
    coup_own[...] = jnp.zeros(coup_own.shape, f32)
    for i in range(4):
        first = GROUP * i + ATOM_DEV
        coup_own[0:4, first : first + ATOM_DEV] = coup_ref[i]

    def coup_copy(k):
        return pltpu.make_async_remote_copy(
            src_ref=coup_own, dst_ref=coup_in.at[k],
            send_sem=coup_send.at[k], recv_sem=coup_recv.at[k],
            device_id=(band, peer((-1, 1)[k])), device_id_type=MESH,
        )

    zero_halo = jnp.zeros((norb, reach_rows, LANES), f32)
    for ext in (ext1, ext2):
        @pl.when(jnp.logical_not(has_left))
        def _():
            ext[:, 0:reach_rows] = zero_halo

        @pl.when(jnp.logical_not(has_right))
        def _():
            ext[:, reach_rows + plane_rows :] = zero_halo

    cell = cell_ref[...]
    atom = atom_ref[...]
    row_of = lax.shift_right_logical(cell, 7)
    lane_of = jnp.bitwise_and(cell, LANES - 1)
    near = jnp.where(atom >= 0, atom - (grid - 1) * ATOM_DEV, -1000)
    for j in range(4):
        hit = lax.broadcasted_iota(jnp.int32, (GROUP, ent), 0) == near
        high, low = split(jnp.where(hit, proj_ref[j : j + 1, :], 0.0))
        m_row[GROUP * j : GROUP * (j + 1)] = high
        m_row[LANES + GROUP * j : LANES + GROUP * (j + 1)] = low
    packed = jnp.concatenate(
        [row_of.astype(f32), lane_of.astype(f32), near.astype(f32), near.astype(f32), proj_ref[...]],
        axis=0,
    )
    cols[...] = packed.T

    @pl.loop(0, ent // TILE)
    def _(i):
        part = pl.ds(pl.multiple_of(i * TILE, TILE), TILE)
        column = cols[part, :]
        lane = lax.broadcasted_iota(jnp.int32, (TILE, LANES), 1).astype(f32)
        wide = lax.broadcasted_iota(jnp.int32, (TILE, plane_rows), 1).astype(f32)
        rows_m[part, :] = jnp.where(column[:, 0:1] == wide, 1.0, 0.0).astype(bf16)
        lane_m[part, :] = jnp.where(column[:, 1:2] == lane, 1.0, 0.0).astype(bf16)

    @pl.when(paired)
    def _():
        pl.semaphore_wait(barrier, n_grid + len(greeted) + 2)

        @pl.loop(0, norb)
        def _(o):
            @pl.when(root)
            def _():
                send_halos(o, 0)

            @pl.when(jnp.logical_not(stays(o)))
            def _():
                swap_copy(o).start()

    @pl.when(root)
    def _():
        filt[0:2] = jnp.zeros((2, plane_rows, LANES), f32)

    for k in range(2):
        coup_copy(k).start()

    apart = jnp.abs(
        lax.broadcasted_iota(jnp.int32, (LANES, LANES), 0)
        - lax.broadcasted_iota(jnp.int32, (LANES, LANES), 1)
    )
    band_m = jnp.zeros((LANES, LANES), f32)
    for k in range(1, REACH + 1):
        band_m = jnp.where(apart == k, EK[k - 1], band_m)
    high, low = split(band_m)
    zmat[0:LANES, 0:LANES] = high
    zmat[0:LANES, LANES:] = low
    zmat[LANES:, 0:LANES] = high
    zmat[LANES:, LANES:] = jnp.zeros((LANES, LANES), bf16)

    def coef_copy(app, b, d):
        return pltpu.make_async_remote_copy(
            src_ref=coef_out.at[app, b], dst_ref=coef_in.at[app, b, d],
            send_sem=coef_send.at[app, b, d], recv_sem=coef_recv.at[app, b, d],
            device_id=(band, peer(COEF_STEPS[d])), device_id_type=MESH,
        )

    def cut(ext, b):
        for x in range(nx):
            high, low = split(ext[b, reach_rows + x * ny : reach_rows + (x + 1) * ny, :])
            vcat[b, x * ny : (x + 1) * ny, 0:LANES] = high
            vcat[b, x * ny : (x + 1) * ny, LANES:] = low

    def coefficients(ext, b, app):
        cut(ext, b)

        row = lax.broadcasted_iota(jnp.int32, (ny, LANES), 0)
        steps = ent // WIDE
        for i in range(steps):
            part = slice(i * WIDE, (i + 1) * WIDE)
            got = dot(rows_m[part, :], vcat[b]).astype(bf16)
            mask = lane_m[part, :]
            picked[part, 0:LANES] = got[:, 0:LANES] * mask
            picked[part, LANES:] = got[:, LANES:] * mask
            for x in range(i * nx // steps, (i + 1) * nx // steps):
                place = slice(x * ny, (x + 1) * ny)
                cells = ext[b, reach_rows + x * ny : reach_rows + (x + 1) * ny, :]
                both = dot(vcat[b, place, :], zmat[...])
                total = both[:, 0:LANES] + both[:, LANES:]
                for k in range(1, REACH + 1):
                    before = jnp.where(row >= k, pltpu.roll(cells, k, 0), 0.0)
                    after = jnp.where(row < ny - k, pltpu.roll(cells, ny - k, 0), 0.0)
                    total = total + EK[k - 1] * (before + after)
                acc[b, place, :] = total

        both = dot(m_row[...], picked[...])
        both = both[0:LANES] + both[LANES:]
        both = (both[:, 0:LANES] + both[:, LANES:]).T
        coef_out[app, b] = jnp.sum(both.reshape(LANES // 8, 8, LANES), axis=0)
        for d in range(len(COEF_STEPS)):
            coef_copy(app, b, d).start()

    lane8 = lax.broadcasted_iota(jnp.int32, (8, LANES), 1)
    slot8 = jnp.bitwise_and(lax.shift_right_logical(lane8, 3), 3)

    def near_total(app, b):
        total = coef_out[app, b]
        for d, step in enumerate(COEF_STEPS):
            coef_copy(app, b, d).wait_recv()
            shift = -step
            there = grid + shift
            lands = slot8 + shift
            keep = (slot8 < 3) & (lands >= 0) & (lands < 3) & (there >= 0) & (there < n_grid)
            total = total + pltpu.roll(
                jnp.where(keep, coef_in[app, b, d], 0.0), (8 * shift) % LANES, 1
            )
        return jnp.broadcast_to(jnp.sum(total, axis=0, keepdims=True), (8, LANES))

    def coupling_rows():
        total = coup_own[...]
        for k, step in enumerate((-1, 1)):
            coup_copy(k).wait_recv()
            shift = -step
            there = grid + shift
            keep = (there >= 0) & (there < n_grid)
            total = total + pltpu.roll(
                jnp.where(keep, coup_in[k], 0.0), (8 * shift) % LANES, 1
            )
        group = lax.shift_right_logical(lax.broadcasted_iota(jnp.int32, (1, LANES), 1), 5)
        for k in range(4):
            line = jnp.zeros((1, LANES), f32)
            for i in range(4):
                j = (i + k) % 4
                line = jnp.where(group == i, total[j : j + 1], line)
            mix[8 * k : 8 * k + 8, :] = jnp.broadcast_to(line * (1.0 / HALF), (8, LANES))

    def inner_terms(ext, b, app):
        near_c = near_total(app, b)
        mixed = mix[0:8, :] * near_c
        for k in range(1, 4):
            mixed = mixed + mix[8 * k : 8 * k + 8, :] * pltpu.roll(near_c, LANES - GROUP * k, 1)
        high, low = split(jnp.broadcast_to(mixed[0:1], (LANES, LANES)).T)
        wcat[0:LANES, 0:LANES] = high
        wcat[0:LANES, LANES:] = low
        wcat[LANES:, 0:LANES] = high
        wcat[LANES:, LANES:] = jnp.zeros((LANES, LANES), bf16)

        for i in range(0, ent, WIDE):
            back = dot(m_col[i : i + WIDE, :], wcat[...])
            high, low = split(back[:, 0:LANES] + back[:, LANES:])
            mask = lane_m[i : i + WIDE, :]
            spread[i : i + WIDE, 0:LANES] = high * mask
            spread[i : i + WIDE, LANES:] = low * mask

        step = 4 * ny

        for i in range(0, plane_rows, step):
            both = dot(rows_t[i : i + step, :], spread[...])
            acc[b, i : i + step, :] = acc[b, i : i + step, :] + (both[:, 0:LANES] + both[:, LANES:])

    def along_x(ext, b, store):
        @pl.loop(0, ny // 8)
        def _(t):
            first = pl.multiple_of(t * 8, 8)
            cells = [
                ext[b, pl.ds(pl.multiple_of(x * ny + first, 8), 8), :]
                for x in range(nx + 2 * REACH)
            ]
            for x in range(nx):
                place = pl.ds(pl.multiple_of(x * ny + first, 8), 8)
                here = cells[x + REACH]
                total = acc[b, place, :] + here * (pot_ref[place, :] * (1.0 / HALF) + DIAG)
                for k in range(1, REACH + 1):
                    total = total + EK[k - 1] * (cells[x + REACH + k] + cells[x + REACH - k])
                store(x, first, place, total)

    def first_coefficients(b):
        own_copy(b).wait()
        coefficients(ext1, b, 0)

    @pl.loop(0, jnp.where(paired, 2, norb))
    def _(b):
        first_coefficients(b)

    @pl.loop(0, ent // TILE)
    def _(i):
        part = pl.ds(pl.multiple_of(i * TILE, TILE), TILE)
        column = cols[part, :]
        lane = lax.broadcasted_iota(jnp.int32, (TILE, LANES), 1).astype(f32)
        total = jnp.zeros((TILE, LANES), f32)
        for j in range(4):
            total = jnp.where(column[:, 2:3] + (GROUP * j) == lane, column[:, 4 + j : 5 + j], total)
        high, low = split(total)
        m_col[part, 0:LANES] = high
        m_col[part, LANES:] = low

    @pl.loop(0, nx)
    def _(x):
        first = pl.multiple_of(x * ny, ny)
        down = lax.broadcasted_iota(jnp.int32, (ny, ent), 0) + first
        rows_t[pl.ds(first, ny), :] = jnp.where(down == row_of, 1.0, 0.0).astype(bf16)

    coupling_rows()
    loads[4].wait()

    def first_application(b):
        inner_terms(ext1, b, 0)
        wait_halos(b, 0, False)

        def store(x, first, place, total):
            ext2[b, pl.ds(pl.multiple_of(reach_rows + x * ny + first, 8), 8), :] = total

        along_x(ext1, b, store)

        @pl.when(jnp.logical_not(follower) | (b == 0))
        def _():
            send_halos(b, 1)

        coefficients(ext2, b, 1)

    def share_of(y):
        return pl.ds(pl.multiple_of(y * share, 8), share)

    def scatter_copy(b, y):
        return pltpu.make_async_remote_copy(
            src_ref=panel.at[b, share_of(y)], dst_ref=panel.at[b, share_of(y)],
            send_sem=scat_send.at[b, y], recv_sem=scat_recv.at[b],
            device_id=(2 * n_zh * y, grid), device_id_type=MESH,
        )

    def z_send_part(b, way, rows):
        return pltpu.make_async_remote_copy(
            src_ref=panel.at[b, rows], dst_ref=panel.at[b, rows],
            send_sem=z_send.at[b, way], recv_sem=z_recv.at[b, way],
            device_id=(along_z(n_zh - 1 if way else 1), grid), device_id_type=MESH,
        )

    def z_copy(b, way):
        return z_send_part(b, way, share_of(yy))

    def z_relay(b, way):
        first = pl.multiple_of(yy * share + way * half, 8)
        return z_send_part(b, way, pl.ds(first, half))

    def y_copy(b, step):
        return pltpu.make_async_remote_copy(
            src_ref=panel.at[b, share_of(yy)], dst_ref=panel.at[b, share_of(yy)],
            send_sem=y_send.at[b, step], recv_sem=y_recv.at[b],
            device_id=(along_y(step), grid), device_id_type=MESH,
        )

    def y_copies(b, act):
        for step in range(1, n_y):
            @pl.when(along_y(step) != 0)
            def _():
                act(y_copy(b, step))

    def sibling_copy(b):
        return pltpu.make_async_remote_copy(
            src_ref=panel.at[b], dst_ref=panel.at[b],
            send_sem=sib_send.at[b], recv_sem=sib_recv.at[b],
            device_id=(sibling, grid), device_id_type=MESH,
        )

    def back_copy(b):
        return pltpu.make_async_remote_copy(
            src_ref=filt.at[b + 2], dst_ref=filt.at[b],
            send_sem=back_send.at[b], recv_sem=back_recv.at[b],
            device_id=(sibling, grid), device_id_type=MESH,
        )

    def start(copy):
        copy.start()

    def z_copies(b, act):
        if ringed:
            for way in range(2):
                act(z_copy(b, way))

    def root_sends(b):
        @pl.when(paired & (b < 2))
        def _():
            q = 2 * core + b
            for y in range(1, n_y):
                scatter_copy(q, y).start()
            z_copies(q, start)
            y_copies(q, start)
            sibling_copy(q).start()

        @pl.when(root & (b >= 2))
        def _():
            back_copy(b - 2).start()

    def phase(k, b):
        if k == 0:
            @pl.when(follower & (zh == 0))
            def _():
                scatter_copy(b, yy).wait_recv()
                z_copies(b, start)
                y_copies(b, start)

        if k == 1 and ringed:
            for z, way in ((1, 0), (3, 1)):
                @pl.when(follower & (zh == z))
                def _():
                    z_copy(b, way).wait_recv()
                    z_relay(b, way).start()
                    y_copies(b, start)

        if k == 2 and ringed:
            @pl.when(follower & (zh == 2))
            def _():
                for way in range(2):
                    z_relay(b, way).wait_recv()
                y_copies(b, start)

        if k == 3:
            @pl.when(follower)
            def _():
                if n_y > 1:
                    most = panel.at[b, pl.ds(0, plane_rows - share)]
                    pltpu.make_async_copy(most, most, y_recv.at[b]).wait()
                sibling_copy(b).start()

    def hand_on(b):
        for k in range(4):
            @pl.when(follower & (b == k))
            def _():
                for q in (0, 2, 1, 3):
                    phase(k, q)
                if k < 3:
                    send_halos(k + 1, 1)

    def second_application(b):
        inner_terms(ext2, b, 1)
        hand_on(b)
        wait_halos(b, 1, False)
        target = jnp.where(paired & (b < 2), norb + 2 * core + b, b)

        def store(x, first, place, total):
            before = ext1[b, pl.ds(pl.multiple_of(reach_rows + x * ny + first, 8), 8), :]
            fields[target, place, :] = 2.0 * total - before

        along_x(ext2, b, store)
        root_sends(b)

        @pl.when(paired & (b == 1))
        def _():
            @pl.when(core == 1)
            def _():
                @pl.loop(0, norb)
                def _(o):
                    send_halos(o, 0)

            @pl.loop(2, norb)
            def _(late):
                first_coefficients(late)

    @pl.loop(0, 2 * norb)
    def _(i):
        first = jnp.where(paired, i % 4 < 2, i < norb)
        b = jnp.where(paired, i // 4 * 2 + i % 2, i % norb)

        @pl.when(first)
        def _():
            first_application(b)

        @pl.when(jnp.logical_not(first))
        def _():
            second_application(b)

    for b in range(norb):
        given = (core == 1) & jnp.logical_not(paired) | paired & (core != b // 2)

        @pl.when(given)
        def _():
            sibling_copy(b).wait_recv()

    @pl.when(band == 1)
    def _():
        for b in range(2):
            back_copy(b).wait_recv()

    couples = [(k, m) for k in range(norb) for m in range(k + 1)]
    n_pairs = len(couples) + norb * norb

    def add_pairs(t, sums):
        place = pl.ds(pl.multiple_of(t * 8, 8), 8)
        p = [panel[k, place, :] for k in range(norb)]
        f = [filt[n, place, :] for n in range(norb)]
        terms = [p[k] * p[m] for k, m in couples] + [p[k] * f[n] for k in range(norb) for n in range(norb)]
        return tuple(s + term for s, term in zip(sums, terms))

    sums = lax.fori_loop(
        0, plane_rows // 8, add_pairs, tuple(jnp.zeros((8, LANES), f32) for _ in range(n_pairs))
    )
    pairs[...] = jnp.zeros(pairs.shape, f32)
    for i, s in enumerate(sums):
        pairs[i : i + 1, :] = jnp.sum(s, axis=0, keepdims=True)
    gram_out[...] = jnp.sum(pairs[...].T.reshape(LANES // 8, 8, LANES), axis=0)

    def gram_copy(step):
        return pltpu.make_async_remote_copy(
            src_ref=gram_out, dst_ref=gram_in.at[step],
            send_sem=gram_send.at[step], recv_sem=gram_recv.at[step],
            device_id=(band, peer(step)), device_id_type=MESH,
        )

    for step in range(1, n_grid):
        gram_copy(step).start()
    total = gram_out[...]
    for step in range(1, n_grid):
        gram_copy(step).wait_recv()
        total = total + gram_in[step]
    total = jnp.sum(total, axis=0, keepdims=True) * (1.0 / (plane_rows * LANES * n_grid))
    lane1 = lax.broadcasted_iota(jnp.int32, (1, LANES), 1)

    def number(i):
        one = jnp.sum(jnp.where(lane1 == i, total, 0.0), axis=1, keepdims=True)
        return jnp.broadcast_to(one, (8, LANES))

    gram = {couple: number(i) for i, couple in enumerate(couples)}
    raw = [[number(len(couples) + k * norb + n) for n in range(norb)] for k in range(norb)]
    lower, inverse = {}, {}
    for j in range(norb):
        left = gram[j, j]
        for m in range(j):
            left = left - lower[j, m] * lower[j, m]
        lower[j, j] = jnp.sqrt(left)
        inverse[j, j] = 1.0 / lower[j, j]
        for i in range(j + 1, norb):
            left = gram[i, j]
            for m in range(j):
                left = left - lower[i, m] * lower[j, m]
            lower[i, j] = left * inverse[j, j]
    for j in range(norb):
        for i in range(j + 1, norb):
            left = lower[i, j] * inverse[j, j]
            for m in range(j + 1, i):
                left = left + lower[i, m] * inverse[m, j]
            inverse[i, j] = -left * inverse[i, i]
    corr = [
        [sum(inverse[k, m] * raw[m][n] for m in range(k + 1)) for n in range(norb)]
        for k in range(norb)
    ]
    weight = [[None] * norb for _ in range(norb)]
    zero8 = jnp.zeros((8, LANES), f32)
    for m in range(norb):
        for n in range(norb):
            away = -sum(inverse[k, m] * corr[k][n] for k in range(m, norb))
            weight[m][n] = jnp.where(root, inverse[n, m] if m <= n else zero8, away)
    keep = jnp.where(root, zero8, jnp.ones((8, LANES), f32))

    @pl.loop(0, plane_rows // 8)
    def _(t):
        place = pl.ds(pl.multiple_of(t * 8, 8), 8)
        p = [panel[k, place, :] for k in range(norb)]
        for n in range(norb):
            value = keep * filt[n, place, :]
            for m in range(norb):
                value = value + weight[m][n] * p[m]
            out_ref[n, place, :] = value

    @pl.loop(0, norb)
    def _(b):
        wait_halos(b, 0, True)
        wait_halos(b, 1, True)
        for app in range(2):
            for d in range(len(COEF_STEPS)):
                coef_copy(app, b, d).wait_send()

        def ended(copy):
            copy.wait_send()

        @pl.when(paired & (core == b // 2))
        def _():
            for y in range(1, n_y):
                scatter_copy(b, y).wait_send()
            z_copies(b, ended)
            y_copies(b, ended)
            sibling_copy(b).wait_send()

        @pl.when(follower)
        def _():
            @pl.when(zh == 0)
            def _():
                z_copies(b, ended)

            if ringed:
                for z, way in ((1, 0), (3, 1)):
                    @pl.when(zh == z)
                    def _():
                        z_relay(b, way).wait_send()

            y_copies(b, ended)
            sibling_copy(b).wait_send()

        @pl.when(jnp.logical_not(stays(b)))
        def _():
            swap_copy(b).wait_send()

        @pl.when(root & (b < 2))
        def _():
            back_copy(b).wait_send()

    for k in range(2):
        coup_copy(k).wait_send()
    for step in range(1, n_grid):
        gram_copy(step).wait_send()


def local(n_band, n_grid, orbitals, potential, projectors, coupling, entry_cell, entry_atom):
    norb, nx, ny, nz = orbitals.shape
    ent = entry_cell.shape[0]
    rows = nx * ny
    chips = n_band // 2
    f32, bf16 = jnp.float32, jnp.bfloat16
    vmem, dma = pltpu.VMEM, pltpu.SemaphoreType.DMA
    ext_rows = rows + 2 * REACH * ny
    whole = pl.BlockSpec(memory_space=pltpu.VMEM)
    out = pl.pallas_call(
        functools.partial(kernel, n_band, n_grid, nx, ny, ent),
        out_shape=jax.ShapeDtypeStruct((norb, rows, nz), f32),
        in_specs=[pl.BlockSpec(memory_space=pltpu.HBM)] * 6,
        out_specs=whole,
        scratch_shapes=[
            vmem((rows, nz), f32),
            vmem(projectors.shape, f32),
            vmem((4, 4, ATOM_DEV), f32),
            vmem((1, ent), jnp.int32),
            vmem((1, ent), jnp.int32),
            vmem((norb, ext_rows, nz), f32),
            vmem((norb, ext_rows, nz), f32),
            vmem((2 * norb, rows, nz), f32),
            vmem((ent, rows), bf16),
            vmem((rows, ent), bf16),
            vmem((ent, LANES), bf16),
            vmem((2 * LANES, ent), bf16),
            vmem((ent, 2 * LANES), bf16),
            vmem((ent, 2 * LANES), bf16),
            vmem((ent, 2 * LANES), bf16),
            vmem((norb, rows, 2 * LANES), bf16),
            vmem((norb, rows, LANES), f32),
            vmem((2 * LANES, 2 * LANES), bf16),
            vmem((2 * LANES, 2 * LANES), bf16),
            vmem((ent, 8), f32),
            vmem((2, norb, 8, LANES), f32),
            vmem((2, norb, 4, 8, LANES), f32),
            vmem((8, LANES), f32),
            vmem((2, 8, LANES), f32),
            vmem((32, LANES), f32),
            vmem((LANES, LANES), f32),
            vmem((8, LANES), f32),
            vmem((n_grid, 8, LANES), f32),
            dma((5,)),
            dma((norb,)),
            dma((norb,)), dma((2,)), dma((2,)),
            dma((2, norb, 2)), dma((2, norb, 2)),
            dma((2, norb, 4)), dma((2, norb, 4)),
            dma((2,)), dma((2,)),
            dma((norb, 4)), dma((norb,)),
            dma((norb, 2)), dma((norb, 2)),
            dma((norb, 4)), dma((norb,)),
            dma((norb,)), dma((norb,)),
            dma((n_grid,)), dma((n_grid,)),
        ],
        compiler_params=pltpu.CompilerParams(
            collective_id=0, has_side_effects=True, vmem_limit_bytes=40 * 1024 * 1024
        ),
        name="filter_panel",
    )(
        *[pltpu.with_memory_space_constraint(v, pltpu.HBM) for v in (orbitals.reshape(norb, rows, nz),
        potential.reshape(rows, nz),
        projectors,
        coupling.transpose(1, 2, 0),
        entry_cell.reshape(1, ent),
        entry_atom.reshape(1, ent))]
    )
    return out.reshape(orbitals.shape)


def solution(mesh):
    return jax.shard_map(
        functools.partial(local, mesh.shape["band"], mesh.shape["grid"]),
        mesh=mesh,
        in_specs=(
            P("band", "grid", None, None),
            P("grid", None, None),
            P(None, "grid"),
            P("grid", None, None),
            P("grid"),
            P("grid"),
        ),
        out_specs=P("band", "grid", None, None),
        check_vma=False,
    )
```

```python
import functools
import math

import jax
import jax.numpy as jnp
from jax import lax
from jax.experimental import pallas as pl
from jax.experimental.pallas import tpu as pltpu
from jax.sharding import PartitionSpec as P

CENTER = 34.0
HALF = 30.0
SPACING = 0.5
REACH = 6
LANES = 128
ATOM_DEV = 8
GROUP = 32
TILE = 256
WIDE = 512
MESH = pl.DeviceIdType.MESH
COEF_STEPS = (-2, -1, 1, 2)


def stencil_weights():
    fact = math.factorial
    side = [
        2.0 * (-1.0) ** (k + 1) * fact(REACH) ** 2 / (k * k * fact(REACH - k) * fact(REACH + k))
        for k in range(1, REACH + 1)
    ]
    return -2.0 * sum(side), side


C0, CK = stencil_weights()
KIN = -0.5 / (SPACING * SPACING)
DIAG = (3.0 * KIN * C0 - CENTER) / HALF
EK = [KIN * c / HALF for c in CK]


def split(x):
    high = x.astype(jnp.bfloat16)
    return high, (x - high.astype(jnp.float32)).astype(jnp.bfloat16)


def dot(a, b):
    return jnp.dot(a, b, preferred_element_type=jnp.float32)


def kernel(
    n_band, n_grid, nx, ny, ent,
    orb_ref, pot_hbm, proj_hbm, coup_hbm, cell_hbm, atom_hbm,
    out_ref,
    pot_ref, proj_ref, coup_ref, cell_ref, atom_ref,
    ext1, ext2, fields, rows_m, rows_t, lane_m, m_row, m_col, picked, spread, vcat, acc,
    zmat, wcat, cols, coef_out, coef_in, coup_own, coup_in, mix, pairs, gram_out, gram_in,
    load_sem, own_sem, swap_send, back_send, back_recv, halo_send, halo_recv, coef_send, coef_recv, coup_send, coup_recv,
    scat_send, scat_recv, z_send, z_recv, z2_send, z2_recv, y_send, y_recv, sib_send, sib_recv,
    gram_send, gram_recv,
):
    f32, bf16 = jnp.float32, jnp.bfloat16
    norb = orb_ref.shape[0]
    plane_rows = nx * ny
    reach_rows = REACH * ny
    chips = n_band // 2
    n_zh = 4 if chips % 4 == 0 else 1
    n_y = chips // n_zh
    ringed = n_zh > 1
    share = plane_rows // n_y
    half = share // 2
    band, grid = lax.axis_index("band"), lax.axis_index("grid")
    chip = lax.div(band, 2)
    zh, yy = lax.rem(chip, n_zh), lax.div(chip, n_zh)
    core = lax.rem(band, 2)
    sibling = band + 1 - 2 * core
    main = core == 0
    paired = band < 2
    filt, panel = fields.at[pl.ds(0, norb)], fields.at[pl.ds(norb, norb)]
    has_left, has_right = grid > 0, grid < n_grid - 1

    def peer(step):
        return lax.rem(grid + step + n_grid, n_grid)

    loads = [
        pltpu.make_async_copy(source, there, load_sem.at[i])
        for i, (source, there) in enumerate(
            [
                (cell_hbm, cell_ref), (atom_hbm, atom_ref), (proj_hbm, proj_ref),
                (coup_hbm, coup_ref), (pot_hbm, pot_ref),
            ]
        )
    ]
    for load in loads:
        load.start()

    barrier = pltpu.get_barrier_semaphore()
    for step in range(1, n_grid):
        pl.semaphore_signal(barrier, inc=1, device_id=(band, peer(step)), device_id_type=MESH)
    pl.semaphore_signal(barrier, inc=1, device_id=(sibling, grid), device_id_type=MESH)

    def along_z(step):
        return 2 * (yy * n_zh + lax.rem(zh + step, n_zh))

    def along_y(step):
        return 2 * (lax.rem(yy + step, n_y) * n_zh + zh)

    root = band == 0
    follower = main & jnp.logical_not(root)
    greeted = [along_z(step) for step in (1, n_zh - 1)] if ringed else []
    greeted += [along_y(step) for step in range(1, n_y)]

    @pl.when(main | paired)
    def _():
        for to in greeted:
            pl.semaphore_signal(barrier, inc=1, device_id=(to, grid), device_id_type=MESH)

    beside_root = follower & ((zh == 0) | ((yy == 0) & (zh != 2)))

    @pl.when(beside_root)
    def _():
        pl.semaphore_signal(barrier, inc=1, device_id=(1, grid), device_id_type=MESH)

    @pl.when(paired)
    def _():
        for step in (-1, 1):
            pl.semaphore_signal(
                barrier, inc=1, device_id=(sibling, peer(step)), device_id_type=MESH
            )

    @pl.when(beside_root)
    def _():
        pl.semaphore_wait(barrier, n_grid + len(greeted) + 1)

    @pl.when(follower & jnp.logical_not(beside_root))
    def _():
        pl.semaphore_wait(barrier, n_grid + len(greeted))

    @pl.when((core == 1) & jnp.logical_not(paired))
    def _():
        pl.semaphore_wait(barrier, n_grid)

    def home(o):
        return jnp.where(paired, o // 2, band), jnp.where(paired, o % 2 + 2 * core, o)

    def halo(b, app, side):
        step = -1 if side == 0 else 1
        start = 0 if app == 0 else reach_rows
        first = start if side == 0 else start + plane_rows - reach_rows
        land = reach_rows + plane_rows if side == 0 else 0
        to_band, place = home(b) if app == 0 else (band, b)
        return pltpu.make_async_remote_copy(
            src_ref=(ext2 if app else orb_ref).at[b, pl.ds(first, reach_rows)],
            dst_ref=(ext2 if app else ext1).at[place, pl.ds(land, reach_rows)],
            send_sem=halo_send.at[app, b, side],
            recv_sem=halo_recv.at[app, place, 1 - side],
            device_id=(to_band, grid + step),
            device_id_type=MESH,
        )

    def arrived(b, app, side):
        ext = ext2 if app else ext1
        land = 0 if side == 0 else reach_rows + plane_rows
        there = ext.at[b, pl.ds(land, reach_rows)]
        return pltpu.make_async_copy(there, there, halo_recv.at[app, b, side])

    def send_halos(b, app):
        @pl.when(has_left)
        def _():
            halo(b, app, 0).start()

        @pl.when(has_right)
        def _():
            halo(b, app, 1).start()

    def wait_halos(b, app, sent):
        @pl.when(has_left)
        def _():
            if sent:
                halo(b, app, 0).wait_send()
            else:
                arrived(b, app, 0).wait()

        @pl.when(has_right)
        def _():
            if sent:
                halo(b, app, 1).wait_send()
            else:
                arrived(b, app, 1).wait()

    def own_copy(b):
        return pltpu.make_async_copy(
            orb_ref.at[b], ext1.at[b, pl.ds(reach_rows, plane_rows)], own_sem.at[b]
        )

    def swap_copy(o):
        place = home(o)[1]
        return pltpu.make_async_remote_copy(
            src_ref=orb_ref.at[o], dst_ref=ext1.at[place, pl.ds(reach_rows, plane_rows)],
            send_sem=swap_send.at[o], recv_sem=own_sem.at[place],
            device_id=(sibling, grid), device_id_type=MESH,
        )

    def stays(o):
        return home(o)[0] == band

    @pl.loop(0, norb)
    def _(o):
        @pl.when(stays(o))
        def _():
            place = home(o)[1]
            pltpu.make_async_copy(
                orb_ref.at[o], ext1.at[place, pl.ds(reach_rows, plane_rows)], own_sem.at[place]
            ).start()

        @pl.when(jnp.logical_not(paired))
        def _():
            send_halos(o, 0)

    for load in loads[:4]:
        load.wait()
    coup_own[...] = jnp.zeros(coup_own.shape, f32)
    for i in range(4):
        first = GROUP * i + ATOM_DEV
        coup_own[0:4, first : first + ATOM_DEV] = coup_ref[i]

    def coup_copy(k):
        return pltpu.make_async_remote_copy(
            src_ref=coup_own, dst_ref=coup_in.at[k],
            send_sem=coup_send.at[k], recv_sem=coup_recv.at[k],
            device_id=(band, peer((-1, 1)[k])), device_id_type=MESH,
        )

    zero_halo = jnp.zeros((norb, reach_rows, LANES), f32)
    for ext in (ext1, ext2):
        @pl.when(jnp.logical_not(has_left))
        def _():
            ext[:, 0:reach_rows] = zero_halo

        @pl.when(jnp.logical_not(has_right))
        def _():
            ext[:, reach_rows + plane_rows :] = zero_halo

    cell = cell_ref[...]
    atom = atom_ref[...]
    row_of = lax.shift_right_logical(cell, 7)
    lane_of = jnp.bitwise_and(cell, LANES - 1)
    near = jnp.where(atom >= 0, atom - (grid - 1) * ATOM_DEV, -1000)
    for j in range(4):
        hit = lax.broadcasted_iota(jnp.int32, (GROUP, ent), 0) == near
        high, low = split(jnp.where(hit, proj_ref[j : j + 1, :], 0.0))
        m_row[GROUP * j : GROUP * (j + 1)] = high
        m_row[LANES + GROUP * j : LANES + GROUP * (j + 1)] = low
    packed = jnp.concatenate(
        [row_of.astype(f32), lane_of.astype(f32), near.astype(f32), near.astype(f32), proj_ref[...]],
        axis=0,
    )
    cols[...] = packed.T

    @pl.loop(0, ent // TILE)
    def _(i):
        part = pl.ds(pl.multiple_of(i * TILE, TILE), TILE)
        column = cols[part, :]
        lane = lax.broadcasted_iota(jnp.int32, (TILE, LANES), 1).astype(f32)
        wide = lax.broadcasted_iota(jnp.int32, (TILE, plane_rows), 1).astype(f32)
        rows_m[part, :] = jnp.where(column[:, 0:1] == wide, 1.0, 0.0).astype(bf16)
        lane_m[part, :] = jnp.where(column[:, 1:2] == lane, 1.0, 0.0).astype(bf16)

    @pl.when(paired)
    def _():
        pl.semaphore_wait(barrier, n_grid + len(greeted) + 2)

        @pl.loop(0, norb)
        def _(o):
            @pl.when(root)
            def _():
                send_halos(o, 0)

            @pl.when(jnp.logical_not(stays(o)))
            def _():
                swap_copy(o).start()

    @pl.when(root)
    def _():
        filt[0:2] = jnp.zeros((2, plane_rows, LANES), f32)

    for k in range(2):
        coup_copy(k).start()

    apart = jnp.abs(
        lax.broadcasted_iota(jnp.int32, (LANES, LANES), 0)
        - lax.broadcasted_iota(jnp.int32, (LANES, LANES), 1)
    )
    band_m = jnp.zeros((LANES, LANES), f32)
    for k in range(1, REACH + 1):
        band_m = jnp.where(apart == k, EK[k - 1], band_m)
    high, low = split(band_m)
    zmat[0:LANES, 0:LANES] = high
    zmat[0:LANES, LANES:] = low
    zmat[LANES:, 0:LANES] = high
    zmat[LANES:, LANES:] = jnp.zeros((LANES, LANES), bf16)

    def coef_copy(app, b, d):
        return pltpu.make_async_remote_copy(
            src_ref=coef_out.at[app, b], dst_ref=coef_in.at[app, b, d],
            send_sem=coef_send.at[app, b, d], recv_sem=coef_recv.at[app, b, d],
            device_id=(band, peer(COEF_STEPS[d])), device_id_type=MESH,
        )

    def cut(ext, b):
        for x in range(nx):
            high, low = split(ext[b, reach_rows + x * ny : reach_rows + (x + 1) * ny, :])
            vcat[b, x * ny : (x + 1) * ny, 0:LANES] = high
            vcat[b, x * ny : (x + 1) * ny, LANES:] = low

    def coefficients(ext, b, app):
        cut(ext, b)

        row = lax.broadcasted_iota(jnp.int32, (ny, LANES), 0)
        steps = ent // WIDE
        for i in range(steps):
            part = slice(i * WIDE, (i + 1) * WIDE)
            got = dot(rows_m[part, :], vcat[b]).astype(bf16)
            mask = lane_m[part, :]
            picked[part, 0:LANES] = got[:, 0:LANES] * mask
            picked[part, LANES:] = got[:, LANES:] * mask
            for x in range(i * nx // steps, (i + 1) * nx // steps):
                place = slice(x * ny, (x + 1) * ny)
                cells = ext[b, reach_rows + x * ny : reach_rows + (x + 1) * ny, :]
                both = dot(vcat[b, place, :], zmat[...])
                total = both[:, 0:LANES] + both[:, LANES:]
                for k in range(1, REACH + 1):
                    before = jnp.where(row >= k, pltpu.roll(cells, k, 0), 0.0)
                    after = jnp.where(row < ny - k, pltpu.roll(cells, ny - k, 0), 0.0)
                    total = total + EK[k - 1] * (before + after)
                acc[b, place, :] = total

        both = dot(m_row[...], picked[...])
        both = both[0:LANES] + both[LANES:]
        both = (both[:, 0:LANES] + both[:, LANES:]).T
        coef_out[app, b] = jnp.sum(both.reshape(LANES // 8, 8, LANES), axis=0)
        for d in range(len(COEF_STEPS)):
            coef_copy(app, b, d).start()

    lane8 = lax.broadcasted_iota(jnp.int32, (8, LANES), 1)
    slot8 = jnp.bitwise_and(lax.shift_right_logical(lane8, 3), 3)

    def near_total(app, b):
        total = coef_out[app, b]
        for d, step in enumerate(COEF_STEPS):
            coef_copy(app, b, d).wait_recv()
            shift = -step
            there = grid + shift
            lands = slot8 + shift
            keep = (slot8 < 3) & (lands >= 0) & (lands < 3) & (there >= 0) & (there < n_grid)
            total = total + pltpu.roll(
                jnp.where(keep, coef_in[app, b, d], 0.0), (8 * shift) % LANES, 1
            )
        return jnp.broadcast_to(jnp.sum(total, axis=0, keepdims=True), (8, LANES))

    def coupling_rows():
        total = coup_own[...]
        for k, step in enumerate((-1, 1)):
            coup_copy(k).wait_recv()
            shift = -step
            there = grid + shift
            keep = (there >= 0) & (there < n_grid)
            total = total + pltpu.roll(
                jnp.where(keep, coup_in[k], 0.0), (8 * shift) % LANES, 1
            )
        group = lax.shift_right_logical(lax.broadcasted_iota(jnp.int32, (1, LANES), 1), 5)
        for k in range(4):
            line = jnp.zeros((1, LANES), f32)
            for i in range(4):
                j = (i + k) % 4
                line = jnp.where(group == i, total[j : j + 1], line)
            mix[8 * k : 8 * k + 8, :] = jnp.broadcast_to(line * (1.0 / HALF), (8, LANES))

    def inner_terms(ext, b, app):
        near_c = near_total(app, b)
        mixed = mix[0:8, :] * near_c
        for k in range(1, 4):
            mixed = mixed + mix[8 * k : 8 * k + 8, :] * pltpu.roll(near_c, LANES - GROUP * k, 1)
        high, low = split(jnp.broadcast_to(mixed[0:1], (LANES, LANES)).T)
        wcat[0:LANES, 0:LANES] = high
        wcat[0:LANES, LANES:] = low
        wcat[LANES:, 0:LANES] = high
        wcat[LANES:, LANES:] = jnp.zeros((LANES, LANES), bf16)

        for i in range(0, ent, WIDE):
            back = dot(m_col[i : i + WIDE, :], wcat[...])
            high, low = split(back[:, 0:LANES] + back[:, LANES:])
            mask = lane_m[i : i + WIDE, :]
            spread[i : i + WIDE, 0:LANES] = high * mask
            spread[i : i + WIDE, LANES:] = low * mask

        step = 4 * ny

        for i in range(0, plane_rows, step):
            both = dot(rows_t[i : i + step, :], spread[...])
            acc[b, i : i + step, :] = acc[b, i : i + step, :] + (both[:, 0:LANES] + both[:, LANES:])

    def along_x(ext, b, store):
        @pl.loop(0, ny // 8)
        def _(t):
            first = pl.multiple_of(t * 8, 8)
            cells = [
                ext[b, pl.ds(pl.multiple_of(x * ny + first, 8), 8), :]
                for x in range(nx + 2 * REACH)
            ]
            for x in range(nx):
                place = pl.ds(pl.multiple_of(x * ny + first, 8), 8)
                here = cells[x + REACH]
                total = acc[b, place, :] + here * (pot_ref[place, :] * (1.0 / HALF) + DIAG)
                for k in range(1, REACH + 1):
                    total = total + EK[k - 1] * (cells[x + REACH + k] + cells[x + REACH - k])
                store(x, first, place, total)

    def first_coefficients(b):
        own_copy(b).wait()
        coefficients(ext1, b, 0)

    @pl.loop(0, jnp.where(paired, 2, norb))
    def _(b):
        first_coefficients(b)

    @pl.loop(0, ent // TILE)
    def _(i):
        part = pl.ds(pl.multiple_of(i * TILE, TILE), TILE)
        column = cols[part, :]
        lane = lax.broadcasted_iota(jnp.int32, (TILE, LANES), 1).astype(f32)
        total = jnp.zeros((TILE, LANES), f32)
        for j in range(4):
            total = jnp.where(column[:, 2:3] + (GROUP * j) == lane, column[:, 4 + j : 5 + j], total)
        high, low = split(total)
        m_col[part, 0:LANES] = high
        m_col[part, LANES:] = low

    @pl.loop(0, nx)
    def _(x):
        first = pl.multiple_of(x * ny, ny)
        down = lax.broadcasted_iota(jnp.int32, (ny, ent), 0) + first
        rows_t[pl.ds(first, ny), :] = jnp.where(down == row_of, 1.0, 0.0).astype(bf16)

    coupling_rows()
    loads[4].wait()

    def first_application(b):
        inner_terms(ext1, b, 0)
        wait_halos(b, 0, False)

        def store(x, first, place, total):
            ext2[b, pl.ds(pl.multiple_of(reach_rows + x * ny + first, 8), 8), :] = total

        along_x(ext1, b, store)

        @pl.when(jnp.logical_not(follower) | (zh == 2) | (b == 0) | ((zh != 0) & (b == 1)))
        def _():
            send_halos(b, 1)

        coefficients(ext2, b, 1)

    def share_of(y):
        return pl.ds(pl.multiple_of(y * share, 8), share)

    def scatter_copy(b, y):
        return pltpu.make_async_remote_copy(
            src_ref=panel.at[b, share_of(y)], dst_ref=panel.at[b, share_of(y)],
            send_sem=scat_send.at[b, y], recv_sem=scat_recv.at[b],
            device_id=(2 * n_zh * y, grid), device_id_type=MESH,
        )

    def z_part(b, way, part, sent, got):
        first = pl.multiple_of(yy * share + part * half, 8)
        rows = pl.ds(first, half)
        return pltpu.make_async_remote_copy(
            src_ref=panel.at[b, rows], dst_ref=panel.at[b, rows],
            send_sem=sent.at[b, way], recv_sem=got.at[b, way],
            device_id=(along_z(n_zh - 1 if way else 1), grid), device_id_type=MESH,
        )

    def z_copy(b, way):
        return z_part(b, way, way, z_send, z_recv)

    def z_second(b, way):
        return z_part(b, way, 1 - way, z2_send, z2_recv)

    def y_copy(b, step):
        return pltpu.make_async_remote_copy(
            src_ref=panel.at[b, share_of(yy)], dst_ref=panel.at[b, share_of(yy)],
            send_sem=y_send.at[b, step], recv_sem=y_recv.at[b],
            device_id=(along_y(step), grid), device_id_type=MESH,
        )

    def y_copies(b, act):
        for step in range(1, n_y):
            @pl.when(along_y(step) != 0)
            def _():
                act(y_copy(b, step))

    def sibling_copy(b):
        return pltpu.make_async_remote_copy(
            src_ref=panel.at[b], dst_ref=panel.at[b],
            send_sem=sib_send.at[b], recv_sem=sib_recv.at[b],
            device_id=(sibling, grid), device_id_type=MESH,
        )

    def back_copy(b):
        return pltpu.make_async_remote_copy(
            src_ref=filt.at[b + 2], dst_ref=filt.at[b],
            send_sem=back_send.at[b], recv_sem=back_recv.at[b],
            device_id=(sibling, grid), device_id_type=MESH,
        )

    def start(copy):
        copy.start()

    def z_copies(b, act):
        if ringed:
            for way in range(2):
                act(z_copy(b, way))
            for way in range(2):
                act(z_second(b, way))

    def root_sends(b):
        @pl.when(paired & (b < 2))
        def _():
            q = 2 * core + b
            for y in range(1, n_y):
                scatter_copy(q, y).start()
            z_copies(q, start)
            y_copies(q, start)
            sibling_copy(q).start()

        @pl.when(root & (b >= 2))
        def _():
            back_copy(b - 2).start()

    turns = (0, 2, 1, 3)

    def hand_on_first(b):
        @pl.when(follower & (zh == 0) & (b == 0))
        def _():
            for q in turns:
                scatter_copy(q, yy).wait_recv()
                if ringed:
                    for way in range(2):
                        z_copy(q, way).start()
            if ringed:
                for q in turns:
                    for way in range(2):
                        z_second(q, way).start()
            for late in range(1, norb):
                send_halos(late, 1)
            for q in turns:
                y_copies(q, start)

    def hand_on_next(b):
        if ringed:
            for z, way in ((1, 0), (3, 1)):
                @pl.when(follower & (zh == z) & (b == 0))
                def _():
                    for q in turns:
                        z_copy(q, way).wait_recv()
                        z_copy(q, way).start()
                    for late in range(2, norb):
                        send_halos(late, 1)
                    for q in turns:
                        z_second(q, way).wait_recv()
                        y_copies(q, start)

            @pl.when(follower & (zh == 2) & (b == 1))
            def _():
                for q in turns:
                    for way in range(2):
                        z_copy(q, way).wait_recv()
                    y_copies(q, start)

    def hand_on_last(b):
        @pl.when(follower & (b == 3))
        def _():
            for q in turns:
                if n_y > 1:
                    most = panel.at[q, pl.ds(0, plane_rows - share)]
                    pltpu.make_async_copy(most, most, y_recv.at[q]).wait()
                sibling_copy(q).start()

    def second_application(b):
        hand_on_first(b)
        inner_terms(ext2, b, 1)
        hand_on_last(b)
        wait_halos(b, 1, False)
        target = jnp.where(paired & (b < 2), norb + 2 * core + b, b)

        def store(x, first, place, total):
            before = ext1[b, pl.ds(pl.multiple_of(reach_rows + x * ny + first, 8), 8), :]
            fields[target, place, :] = 2.0 * total - before

        along_x(ext2, b, store)
        root_sends(b)
        hand_on_next(b)

        @pl.when(paired & (b == 1))
        def _():
            @pl.when(core == 1)
            def _():
                @pl.loop(0, norb)
                def _(o):
                    send_halos(o, 0)

            @pl.loop(2, norb)
            def _(late):
                first_coefficients(late)

    @pl.loop(0, 2 * norb)
    def _(i):
        first = jnp.where(paired, i % 4 < 2, i < norb)
        b = jnp.where(paired, i // 4 * 2 + i % 2, i % norb)

        @pl.when(first)
        def _():
            first_application(b)

        @pl.when(jnp.logical_not(first))
        def _():
            second_application(b)

    for b in range(norb):
        given = (core == 1) & jnp.logical_not(paired) | paired & (core != b // 2)

        @pl.when(given)
        def _():
            sibling_copy(b).wait_recv()

    @pl.when(band == 1)
    def _():
        for b in range(2):
            back_copy(b).wait_recv()

    couples = [(k, m) for k in range(norb) for m in range(k + 1)]
    n_pairs = len(couples) + norb * norb

    def add_pairs(t, sums):
        place = pl.ds(pl.multiple_of(t * 8, 8), 8)
        p = [panel[k, place, :] for k in range(norb)]
        f = [filt[n, place, :] for n in range(norb)]
        terms = [p[k] * p[m] for k, m in couples] + [p[k] * f[n] for k in range(norb) for n in range(norb)]
        return tuple(s + term for s, term in zip(sums, terms))

    sums = lax.fori_loop(
        0, plane_rows // 8, add_pairs, tuple(jnp.zeros((8, LANES), f32) for _ in range(n_pairs))
    )
    pairs[...] = jnp.zeros(pairs.shape, f32)
    for i, s in enumerate(sums):
        pairs[i : i + 1, :] = jnp.sum(s, axis=0, keepdims=True)
    gram_out[...] = jnp.sum(pairs[...].T.reshape(LANES // 8, 8, LANES), axis=0)

    def gram_copy(step):
        return pltpu.make_async_remote_copy(
            src_ref=gram_out, dst_ref=gram_in.at[step],
            send_sem=gram_send.at[step], recv_sem=gram_recv.at[step],
            device_id=(band, peer(step)), device_id_type=MESH,
        )

    for step in range(1, n_grid):
        gram_copy(step).start()
    total = gram_out[...]
    for step in range(1, n_grid):
        gram_copy(step).wait_recv()
        total = total + gram_in[step]
    total = jnp.sum(total, axis=0, keepdims=True) * (1.0 / (plane_rows * LANES * n_grid))
    lane1 = lax.broadcasted_iota(jnp.int32, (1, LANES), 1)

    def number(i):
        one = jnp.sum(jnp.where(lane1 == i, total, 0.0), axis=1, keepdims=True)
        return jnp.broadcast_to(one, (8, LANES))

    gram = {couple: number(i) for i, couple in enumerate(couples)}
    raw = [[number(len(couples) + k * norb + n) for n in range(norb)] for k in range(norb)]
    lower, inverse = {}, {}
    for j in range(norb):
        left = gram[j, j]
        for m in range(j):
            left = left - lower[j, m] * lower[j, m]
        lower[j, j] = jnp.sqrt(left)
        inverse[j, j] = 1.0 / lower[j, j]
        for i in range(j + 1, norb):
            left = gram[i, j]
            for m in range(j):
                left = left - lower[i, m] * lower[j, m]
            lower[i, j] = left * inverse[j, j]
    for j in range(norb):
        for i in range(j + 1, norb):
            left = lower[i, j] * inverse[j, j]
            for m in range(j + 1, i):
                left = left + lower[i, m] * inverse[m, j]
            inverse[i, j] = -left * inverse[i, i]
    corr = [
        [sum(inverse[k, m] * raw[m][n] for m in range(k + 1)) for n in range(norb)]
        for k in range(norb)
    ]
    weight = [[None] * norb for _ in range(norb)]
    zero8 = jnp.zeros((8, LANES), f32)
    for m in range(norb):
        for n in range(norb):
            away = -sum(inverse[k, m] * corr[k][n] for k in range(m, norb))
            weight[m][n] = jnp.where(root, inverse[n, m] if m <= n else zero8, away)
    keep = jnp.where(root, zero8, jnp.ones((8, LANES), f32))

    @pl.loop(0, plane_rows // 8)
    def _(t):
        place = pl.ds(pl.multiple_of(t * 8, 8), 8)
        p = [panel[k, place, :] for k in range(norb)]
        for n in range(norb):
            value = keep * filt[n, place, :]
            for m in range(norb):
                value = value + weight[m][n] * p[m]
            out_ref[n, place, :] = value

    @pl.loop(0, norb)
    def _(b):
        wait_halos(b, 0, True)
        wait_halos(b, 1, True)
        for app in range(2):
            for d in range(len(COEF_STEPS)):
                coef_copy(app, b, d).wait_send()

        def ended(copy):
            copy.wait_send()

        @pl.when(paired & (core == b // 2))
        def _():
            for y in range(1, n_y):
                scatter_copy(b, y).wait_send()
            z_copies(b, ended)
            y_copies(b, ended)
            sibling_copy(b).wait_send()

        @pl.when(follower)
        def _():
            @pl.when(zh == 0)
            def _():
                z_copies(b, ended)

            if ringed:
                for z, way in ((1, 0), (3, 1)):
                    @pl.when(zh == z)
                    def _():
                        z_copy(b, way).wait_send()

            y_copies(b, ended)
            sibling_copy(b).wait_send()

        @pl.when(jnp.logical_not(stays(b)))
        def _():
            swap_copy(b).wait_send()

        @pl.when(root & (b < 2))
        def _():
            back_copy(b).wait_send()

    for k in range(2):
        coup_copy(k).wait_send()
    for step in range(1, n_grid):
        gram_copy(step).wait_send()


def local(n_band, n_grid, orbitals, potential, projectors, coupling, entry_cell, entry_atom):
    norb, nx, ny, nz = orbitals.shape
    ent = entry_cell.shape[0]
    rows = nx * ny
    chips = n_band // 2
    f32, bf16 = jnp.float32, jnp.bfloat16
    vmem, dma = pltpu.VMEM, pltpu.SemaphoreType.DMA
    ext_rows = rows + 2 * REACH * ny
    whole = pl.BlockSpec(memory_space=pltpu.VMEM)
    out = pl.pallas_call(
        functools.partial(kernel, n_band, n_grid, nx, ny, ent),
        out_shape=jax.ShapeDtypeStruct((norb, rows, nz), f32),
        in_specs=[pl.BlockSpec(memory_space=pltpu.HBM)] * 6,
        out_specs=whole,
        scratch_shapes=[
            vmem((rows, nz), f32),
            vmem(projectors.shape, f32),
            vmem((4, 4, ATOM_DEV), f32),
            vmem((1, ent), jnp.int32),
            vmem((1, ent), jnp.int32),
            vmem((norb, ext_rows, nz), f32),
            vmem((norb, ext_rows, nz), f32),
            vmem((2 * norb, rows, nz), f32),
            vmem((ent, rows), bf16),
            vmem((rows, ent), bf16),
            vmem((ent, LANES), bf16),
            vmem((2 * LANES, ent), bf16),
            vmem((ent, 2 * LANES), bf16),
            vmem((ent, 2 * LANES), bf16),
            vmem((ent, 2 * LANES), bf16),
            vmem((norb, rows, 2 * LANES), bf16),
            vmem((norb, rows, LANES), f32),
            vmem((2 * LANES, 2 * LANES), bf16),
            vmem((2 * LANES, 2 * LANES), bf16),
            vmem((ent, 8), f32),
            vmem((2, norb, 8, LANES), f32),
            vmem((2, norb, 4, 8, LANES), f32),
            vmem((8, LANES), f32),
            vmem((2, 8, LANES), f32),
            vmem((32, LANES), f32),
            vmem((LANES, LANES), f32),
            vmem((8, LANES), f32),
            vmem((n_grid, 8, LANES), f32),
            dma((5,)),
            dma((norb,)),
            dma((norb,)), dma((2,)), dma((2,)),
            dma((2, norb, 2)), dma((2, norb, 2)),
            dma((2, norb, 4)), dma((2, norb, 4)),
            dma((2,)), dma((2,)),
            dma((norb, 4)), dma((norb,)),
            dma((norb, 2)), dma((norb, 2)),
            dma((norb, 2)), dma((norb, 2)),
            dma((norb, 4)), dma((norb,)),
            dma((norb,)), dma((norb,)),
            dma((n_grid,)), dma((n_grid,)),
        ],
        compiler_params=pltpu.CompilerParams(
            collective_id=0, has_side_effects=True, vmem_limit_bytes=40 * 1024 * 1024
        ),
        name="filter_panel",
    )(
        *[pltpu.with_memory_space_constraint(v, pltpu.HBM) for v in (orbitals.reshape(norb, rows, nz),
        potential.reshape(rows, nz),
        projectors,
        coupling.transpose(1, 2, 0),
        entry_cell.reshape(1, ent),
        entry_atom.reshape(1, ent))]
    )
    return out.reshape(orbitals.shape)


def solution(mesh):
    return jax.shard_map(
        functools.partial(local, mesh.shape["band"], mesh.shape["grid"]),
        mesh=mesh,
        in_specs=(
            P("band", "grid", None, None),
            P("grid", None, None),
            P(None, "grid"),
            P("grid", None, None),
            P("grid"),
            P("grid"),
        ),
        out_specs=P("band", "grid", None, None),
        check_vma=False,
    )
```

```python
import functools
import math

import jax
import jax.numpy as jnp
from jax import lax
from jax.experimental import pallas as pl
from jax.experimental.pallas import tpu as pltpu
from jax.sharding import PartitionSpec as P

CENTER = 34.0
HALF = 30.0
SPACING = 0.5
REACH = 6
LANES = 128
ATOM_DEV = 8
GROUP = 32
TILE = 256
WIDE = 512
MESH = pl.DeviceIdType.MESH
COEF_STEPS = (-2, -1, 1, 2)


def stencil_weights():
    fact = math.factorial
    side = [
        2.0 * (-1.0) ** (k + 1) * fact(REACH) ** 2 / (k * k * fact(REACH - k) * fact(REACH + k))
        for k in range(1, REACH + 1)
    ]
    return -2.0 * sum(side), side


C0, CK = stencil_weights()
KIN = -0.5 / (SPACING * SPACING)
DIAG = (3.0 * KIN * C0 - CENTER) / HALF
EK = [KIN * c / HALF for c in CK]


def split(x):
    high = x.astype(jnp.bfloat16)
    return high, (x - high.astype(jnp.float32)).astype(jnp.bfloat16)


def dot(a, b):
    return jnp.dot(a, b, preferred_element_type=jnp.float32)


def kernel(
    n_band, n_grid, nx, ny, ent,
    orb_ref, pot_hbm, proj_hbm, coup_hbm, cell_hbm, atom_hbm,
    out_ref,
    pot_ref, proj_ref, coup_ref, cell_ref, atom_ref,
    ext1, ext2, fields, rows_m, rows_t, lane_m, m_row, m_col, picked, spread, vcat, acc,
    zmat, wcat, cols, coef_out, coef_in, coup_own, coup_in, mix, pairs, gram_out, gram_in,
    load_sem, own_sem, swap_send, back_send, back_recv, halo_send, halo_recv, coef_send, coef_recv, coup_send, coup_recv,
    scat_send, scat_recv, z_send, z_recv, z2_send, z2_recv, y_send, y_recv, sib_send, sib_recv,
    gram_send, gram_recv,
):
    f32, bf16 = jnp.float32, jnp.bfloat16
    norb = orb_ref.shape[0]
    plane_rows = nx * ny
    reach_rows = REACH * ny
    chips = n_band // 2
    n_zh = 4 if chips % 4 == 0 else 1
    n_y = chips // n_zh
    ringed = n_zh > 1
    share = plane_rows // n_y
    half = share // 2
    band, grid = lax.axis_index("band"), lax.axis_index("grid")
    chip = lax.div(band, 2)
    zh, yy = lax.rem(chip, n_zh), lax.div(chip, n_zh)
    core = lax.rem(band, 2)
    sibling = band + 1 - 2 * core
    main = core == 0
    paired = band < 2
    filt, panel = fields.at[pl.ds(0, norb)], fields.at[pl.ds(norb, norb)]
    has_left, has_right = grid > 0, grid < n_grid - 1

    def peer(step):
        return lax.rem(grid + step + n_grid, n_grid)

    loads = [
        pltpu.make_async_copy(source, there, load_sem.at[i])
        for i, (source, there) in enumerate(
            [
                (cell_hbm, cell_ref), (atom_hbm, atom_ref), (proj_hbm, proj_ref),
                (coup_hbm, coup_ref), (pot_hbm, pot_ref),
            ]
        )
    ]
    for load in loads:
        load.start()

    barrier = pltpu.get_barrier_semaphore()
    for step in range(1, n_grid):
        pl.semaphore_signal(barrier, inc=1, device_id=(band, peer(step)), device_id_type=MESH)
    pl.semaphore_signal(barrier, inc=1, device_id=(sibling, grid), device_id_type=MESH)

    def along_z(step):
        return 2 * (yy * n_zh + lax.rem(zh + step, n_zh))

    def along_y(step):
        return 2 * (lax.rem(yy + step, n_y) * n_zh + zh)

    root = band == 0
    follower = main & jnp.logical_not(root)
    greeted = [along_z(step) for step in (1, n_zh - 1)] if ringed else []
    greeted += [along_y(step) for step in range(1, n_y)]

    @pl.when(main | paired)
    def _():
        for to in greeted:
            pl.semaphore_signal(barrier, inc=1, device_id=(to, grid), device_id_type=MESH)

    beside_root = follower & ((zh == 0) | ((yy == 0) & (zh != 2)))

    @pl.when(beside_root)
    def _():
        pl.semaphore_signal(barrier, inc=1, device_id=(1, grid), device_id_type=MESH)

    @pl.when(paired)
    def _():
        for step in (-1, 1):
            pl.semaphore_signal(
                barrier, inc=1, device_id=(sibling, peer(step)), device_id_type=MESH
            )

    @pl.when(beside_root)
    def _():
        pl.semaphore_wait(barrier, n_grid + len(greeted) + 1)

    @pl.when(follower & jnp.logical_not(beside_root))
    def _():
        pl.semaphore_wait(barrier, n_grid + len(greeted))

    @pl.when((core == 1) & jnp.logical_not(paired))
    def _():
        pl.semaphore_wait(barrier, n_grid)

    def home(o):
        return jnp.where(paired, o // 2, band), jnp.where(paired, o % 2 + 2 * core, o)

    def halo(b, app, side):
        step = -1 if side == 0 else 1
        start = 0 if app == 0 else reach_rows
        first = start if side == 0 else start + plane_rows - reach_rows
        land = reach_rows + plane_rows if side == 0 else 0
        to_band, place = home(b) if app == 0 else (band, b)
        return pltpu.make_async_remote_copy(
            src_ref=(ext2 if app else orb_ref).at[b, pl.ds(first, reach_rows)],
            dst_ref=(ext2 if app else ext1).at[place, pl.ds(land, reach_rows)],
            send_sem=halo_send.at[app, b, side],
            recv_sem=halo_recv.at[app, place, 1 - side],
            device_id=(to_band, grid + step),
            device_id_type=MESH,
        )

    def arrived(b, app, side):
        ext = ext2 if app else ext1
        land = 0 if side == 0 else reach_rows + plane_rows
        there = ext.at[b, pl.ds(land, reach_rows)]
        return pltpu.make_async_copy(there, there, halo_recv.at[app, b, side])

    def send_halos(b, app):
        @pl.when(has_left)
        def _():
            halo(b, app, 0).start()

        @pl.when(has_right)
        def _():
            halo(b, app, 1).start()

    def wait_halos(b, app, sent):
        @pl.when(has_left)
        def _():
            if sent:
                halo(b, app, 0).wait_send()
            else:
                arrived(b, app, 0).wait()

        @pl.when(has_right)
        def _():
            if sent:
                halo(b, app, 1).wait_send()
            else:
                arrived(b, app, 1).wait()

    def own_copy(b):
        return pltpu.make_async_copy(
            orb_ref.at[b], ext1.at[b, pl.ds(reach_rows, plane_rows)], own_sem.at[b]
        )

    def swap_copy(o):
        place = home(o)[1]
        return pltpu.make_async_remote_copy(
            src_ref=orb_ref.at[o], dst_ref=ext1.at[place, pl.ds(reach_rows, plane_rows)],
            send_sem=swap_send.at[o], recv_sem=own_sem.at[place],
            device_id=(sibling, grid), device_id_type=MESH,
        )

    def stays(o):
        return home(o)[0] == band

    @pl.loop(0, norb)
    def _(o):
        @pl.when(stays(o))
        def _():
            place = home(o)[1]
            pltpu.make_async_copy(
                orb_ref.at[o], ext1.at[place, pl.ds(reach_rows, plane_rows)], own_sem.at[place]
            ).start()

        @pl.when(jnp.logical_not(paired))
        def _():
            send_halos(o, 0)

    for load in loads[:4]:
        load.wait()
    coup_own[...] = jnp.zeros(coup_own.shape, f32)
    for i in range(4):
        first = GROUP * i + ATOM_DEV
        coup_own[0:4, first : first + ATOM_DEV] = coup_ref[i]

    def coup_copy(k):
        return pltpu.make_async_remote_copy(
            src_ref=coup_own, dst_ref=coup_in.at[k],
            send_sem=coup_send.at[k], recv_sem=coup_recv.at[k],
            device_id=(band, peer((-1, 1)[k])), device_id_type=MESH,
        )

    zero_halo = jnp.zeros((norb, reach_rows, LANES), f32)
    for ext in (ext1, ext2):
        @pl.when(jnp.logical_not(has_left))
        def _():
            ext[:, 0:reach_rows] = zero_halo

        @pl.when(jnp.logical_not(has_right))
        def _():
            ext[:, reach_rows + plane_rows :] = zero_halo

    cell = cell_ref[...]
    atom = atom_ref[...]
    row_of = lax.shift_right_logical(cell, 7)
    lane_of = jnp.bitwise_and(cell, LANES - 1)
    near = jnp.where(atom >= 0, atom - (grid - 1) * ATOM_DEV, -1000)
    for j in range(4):
        hit = lax.broadcasted_iota(jnp.int32, (GROUP, ent), 0) == near
        high, low = split(jnp.where(hit, proj_ref[j : j + 1, :], 0.0))
        m_row[GROUP * j : GROUP * (j + 1)] = high
        m_row[LANES + GROUP * j : LANES + GROUP * (j + 1)] = low
    packed = jnp.concatenate(
        [row_of.astype(f32), lane_of.astype(f32), near.astype(f32), near.astype(f32), proj_ref[...]],
        axis=0,
    )
    cols[...] = packed.T

    @pl.loop(0, ent // TILE)
    def _(i):
        part = pl.ds(pl.multiple_of(i * TILE, TILE), TILE)
        column = cols[part, :]
        lane = lax.broadcasted_iota(jnp.int32, (TILE, LANES), 1).astype(f32)
        wide = lax.broadcasted_iota(jnp.int32, (TILE, plane_rows), 1).astype(f32)
        rows_m[part, :] = jnp.where(column[:, 0:1] == wide, 1.0, 0.0).astype(bf16)
        lane_m[part, :] = jnp.where(column[:, 1:2] == lane, 1.0, 0.0).astype(bf16)

    @pl.when(paired)
    def _():
        pl.semaphore_wait(barrier, n_grid + len(greeted) + 2)

        @pl.loop(0, norb)
        def _(o):
            @pl.when(root)
            def _():
                send_halos(o, 0)

            @pl.when(jnp.logical_not(stays(o)))
            def _():
                swap_copy(o).start()

    @pl.when(root)
    def _():
        filt[0:2] = jnp.zeros((2, plane_rows, LANES), f32)

    for k in range(2):
        coup_copy(k).start()

    apart = jnp.abs(
        lax.broadcasted_iota(jnp.int32, (LANES, LANES), 0)
        - lax.broadcasted_iota(jnp.int32, (LANES, LANES), 1)
    )
    band_m = jnp.zeros((LANES, LANES), f32)
    for k in range(1, REACH + 1):
        band_m = jnp.where(apart == k, EK[k - 1], band_m)
    high, low = split(band_m)
    zmat[0:LANES, 0:LANES] = high
    zmat[0:LANES, LANES:] = low
    zmat[LANES:, 0:LANES] = high
    zmat[LANES:, LANES:] = jnp.zeros((LANES, LANES), bf16)

    def coef_copy(app, b, d):
        return pltpu.make_async_remote_copy(
            src_ref=coef_out.at[app, b], dst_ref=coef_in.at[app, b, d],
            send_sem=coef_send.at[app, b, d], recv_sem=coef_recv.at[app, b, d],
            device_id=(band, peer(COEF_STEPS[d])), device_id_type=MESH,
        )

    def cut(ext, b):
        for x in range(nx):
            high, low = split(ext[b, reach_rows + x * ny : reach_rows + (x + 1) * ny, :])
            vcat[b, x * ny : (x + 1) * ny, 0:LANES] = high
            vcat[b, x * ny : (x + 1) * ny, LANES:] = low

    def coefficients(ext, b, app):
        cut(ext, b)

        row = lax.broadcasted_iota(jnp.int32, (ny, LANES), 0)
        steps = ent // WIDE
        for i in range(steps):
            part = slice(i * WIDE, (i + 1) * WIDE)
            got = dot(rows_m[part, :], vcat[b]).astype(bf16)
            mask = lane_m[part, :]
            picked[part, 0:LANES] = got[:, 0:LANES] * mask
            picked[part, LANES:] = got[:, LANES:] * mask
            for x in range(i * nx // steps, (i + 1) * nx // steps):
                place = slice(x * ny, (x + 1) * ny)
                cells = ext[b, reach_rows + x * ny : reach_rows + (x + 1) * ny, :]
                both = dot(vcat[b, place, :], zmat[...])
                total = both[:, 0:LANES] + both[:, LANES:]
                for k in range(1, REACH + 1):
                    before = jnp.where(row >= k, pltpu.roll(cells, k, 0), 0.0)
                    after = jnp.where(row < ny - k, pltpu.roll(cells, ny - k, 0), 0.0)
                    total = total + EK[k - 1] * (before + after)
                acc[b, place, :] = total

        both = dot(m_row[...], picked[...])
        both = both[0:LANES] + both[LANES:]
        both = (both[:, 0:LANES] + both[:, LANES:]).T
        coef_out[app, b] = jnp.sum(both.reshape(LANES // 8, 8, LANES), axis=0)
        for d in range(len(COEF_STEPS)):
            coef_copy(app, b, d).start()

    lane8 = lax.broadcasted_iota(jnp.int32, (8, LANES), 1)
    slot8 = jnp.bitwise_and(lax.shift_right_logical(lane8, 3), 3)

    def near_total(app, b):
        total = coef_out[app, b]
        for d, step in enumerate(COEF_STEPS):
            coef_copy(app, b, d).wait_recv()
            shift = -step
            there = grid + shift
            lands = slot8 + shift
            keep = (slot8 < 3) & (lands >= 0) & (lands < 3) & (there >= 0) & (there < n_grid)
            total = total + pltpu.roll(
                jnp.where(keep, coef_in[app, b, d], 0.0), (8 * shift) % LANES, 1
            )
        return jnp.broadcast_to(jnp.sum(total, axis=0, keepdims=True), (8, LANES))

    def coupling_rows():
        total = coup_own[...]
        for k, step in enumerate((-1, 1)):
            coup_copy(k).wait_recv()
            shift = -step
            there = grid + shift
            keep = (there >= 0) & (there < n_grid)
            total = total + pltpu.roll(
                jnp.where(keep, coup_in[k], 0.0), (8 * shift) % LANES, 1
            )
        group = lax.shift_right_logical(lax.broadcasted_iota(jnp.int32, (1, LANES), 1), 5)
        for k in range(4):
            line = jnp.zeros((1, LANES), f32)
            for i in range(4):
                j = (i + k) % 4
                line = jnp.where(group == i, total[j : j + 1], line)
            mix[8 * k : 8 * k + 8, :] = jnp.broadcast_to(line * (1.0 / HALF), (8, LANES))

    def inner_terms(ext, b, app):
        near_c = near_total(app, b)
        mixed = mix[0:8, :] * near_c
        for k in range(1, 4):
            mixed = mixed + mix[8 * k : 8 * k + 8, :] * pltpu.roll(near_c, LANES - GROUP * k, 1)
        high, low = split(jnp.broadcast_to(mixed[0:1], (LANES, LANES)).T)
        wcat[0:LANES, 0:LANES] = high
        wcat[0:LANES, LANES:] = low
        wcat[LANES:, 0:LANES] = high
        wcat[LANES:, LANES:] = jnp.zeros((LANES, LANES), bf16)

        for i in range(0, ent, WIDE):
            back = dot(m_col[i : i + WIDE, :], wcat[...])
            high, low = split(back[:, 0:LANES] + back[:, LANES:])
            mask = lane_m[i : i + WIDE, :]
            spread[i : i + WIDE, 0:LANES] = high * mask
            spread[i : i + WIDE, LANES:] = low * mask

        step = 4 * ny

        for i in range(0, plane_rows, step):
            both = dot(rows_t[i : i + step, :], spread[...])
            acc[b, i : i + step, :] = acc[b, i : i + step, :] + (both[:, 0:LANES] + both[:, LANES:])

    def along_x(ext, b, store):
        @pl.loop(0, ny // 8)
        def _(t):
            first = pl.multiple_of(t * 8, 8)
            cells = [
                ext[b, pl.ds(pl.multiple_of(x * ny + first, 8), 8), :]
                for x in range(nx + 2 * REACH)
            ]
            for x in range(nx):
                place = pl.ds(pl.multiple_of(x * ny + first, 8), 8)
                here = cells[x + REACH]
                total = acc[b, place, :] + here * (pot_ref[place, :] * (1.0 / HALF) + DIAG)
                for k in range(1, REACH + 1):
                    total = total + EK[k - 1] * (cells[x + REACH + k] + cells[x + REACH - k])
                store(x, first, place, total)

    def first_coefficients(b):
        own_copy(b).wait()
        coefficients(ext1, b, 0)

    @pl.loop(0, jnp.where(paired, 2, norb))
    def _(b):
        first_coefficients(b)

    @pl.loop(0, ent // TILE)
    def _(i):
        part = pl.ds(pl.multiple_of(i * TILE, TILE), TILE)
        column = cols[part, :]
        lane = lax.broadcasted_iota(jnp.int32, (TILE, LANES), 1).astype(f32)
        total = jnp.zeros((TILE, LANES), f32)
        for j in range(4):
            total = jnp.where(column[:, 2:3] + (GROUP * j) == lane, column[:, 4 + j : 5 + j], total)
        high, low = split(total)
        m_col[part, 0:LANES] = high
        m_col[part, LANES:] = low

    @pl.loop(0, nx)
    def _(x):
        first = pl.multiple_of(x * ny, ny)
        down = lax.broadcasted_iota(jnp.int32, (ny, ent), 0) + first
        rows_t[pl.ds(first, ny), :] = jnp.where(down == row_of, 1.0, 0.0).astype(bf16)

    coupling_rows()
    loads[4].wait()

    def first_application(b):
        inner_terms(ext1, b, 0)
        wait_halos(b, 0, False)

        def store(x, first, place, total):
            ext2[b, pl.ds(pl.multiple_of(reach_rows + x * ny + first, 8), 8), :] = total

        along_x(ext1, b, store)

        @pl.when(jnp.logical_not(follower) | ((zh == 2) & (b < 3)) | (b == 0) | ((zh != 0) & (b == 1)))
        def _():
            send_halos(b, 1)

        coefficients(ext2, b, 1)

    def share_of(y):
        return pl.ds(pl.multiple_of(y * share, 8), share)

    def scatter_copy(b, y):
        return pltpu.make_async_remote_copy(
            src_ref=panel.at[b, share_of(y)], dst_ref=panel.at[b, share_of(y)],
            send_sem=scat_send.at[b, y], recv_sem=scat_recv.at[b],
            device_id=(2 * n_zh * y, grid), device_id_type=MESH,
        )

    def z_part(b, way, part, sent, got):
        first = pl.multiple_of(yy * share + part * half, 8)
        rows = pl.ds(first, half)
        return pltpu.make_async_remote_copy(
            src_ref=panel.at[b, rows], dst_ref=panel.at[b, rows],
            send_sem=sent.at[b, way], recv_sem=got.at[b, way],
            device_id=(along_z(n_zh - 1 if way else 1), grid), device_id_type=MESH,
        )

    def z_copy(b, way):
        return z_part(b, way, way, z_send, z_recv)

    def z_second(b, way):
        return z_part(b, way, 1 - way, z2_send, z2_recv)

    def y_copy(b, step):
        return pltpu.make_async_remote_copy(
            src_ref=panel.at[b, share_of(yy)], dst_ref=panel.at[b, share_of(yy)],
            send_sem=y_send.at[b, step], recv_sem=y_recv.at[b],
            device_id=(along_y(step), grid), device_id_type=MESH,
        )

    def y_copies(b, act):
        for step in sorted(range(1, n_y), key=lambda step: abs(2 * step - n_y)):
            @pl.when(along_y(step) != 0)
            def _():
                act(y_copy(b, step))

    def sibling_copy(b):
        return pltpu.make_async_remote_copy(
            src_ref=panel.at[b], dst_ref=panel.at[b],
            send_sem=sib_send.at[b], recv_sem=sib_recv.at[b],
            device_id=(sibling, grid), device_id_type=MESH,
        )

    def back_copy(b):
        return pltpu.make_async_remote_copy(
            src_ref=filt.at[b + 2], dst_ref=filt.at[b],
            send_sem=back_send.at[b], recv_sem=back_recv.at[b],
            device_id=(sibling, grid), device_id_type=MESH,
        )

    def start(copy):
        copy.start()

    def z_copies(b, act):
        if ringed:
            for way in range(2):
                act(z_copy(b, way))
            for way in range(2):
                act(z_second(b, way))

    def root_sends(b):
        @pl.when(paired & (b < 2))
        def _():
            q = 2 * core + b
            for y in range(1, n_y):
                scatter_copy(q, y).start()
            z_copies(q, start)
            y_copies(q, start)
            sibling_copy(q).start()

        @pl.when(root & (b >= 2))
        def _():
            back_copy(b - 2).start()

    turns = (0, 2, 1, 3)

    def hand_on_first(b):
        @pl.when(follower & (zh == 0) & (b == 0))
        def _():
            for q in turns:
                scatter_copy(q, yy).wait_recv()
                if ringed:
                    for way in range(2):
                        z_copy(q, way).start()
            if ringed:
                for q in turns:
                    for way in range(2):
                        z_second(q, way).start()
            for late in range(1, norb):
                send_halos(late, 1)
            for q in turns:
                y_copies(q, start)

    def hand_on_next(b):
        if ringed:
            for z, way in ((1, 0), (3, 1)):
                @pl.when(follower & (zh == z) & (b == 0))
                def _():
                    for q in turns:
                        z_copy(q, way).wait_recv()
                        z_copy(q, way).start()
                    for late in range(2, norb):
                        send_halos(late, 1)
                    for q in turns:
                        z_second(q, way).wait_recv()
                        y_copies(q, start)

            @pl.when(follower & (zh == 2) & (b == 1))
            def _():
                for q in turns:
                    for way in range(2):
                        z_copy(q, way).wait_recv()
                    y_copies(q, start)
                send_halos(3, 1)

    def hand_on_last(b):
        @pl.when(follower & (b == 3))
        def _():
            for q in turns:
                if n_y > 1:
                    most = panel.at[q, pl.ds(0, plane_rows - share)]
                    pltpu.make_async_copy(most, most, y_recv.at[q]).wait()
                sibling_copy(q).start()

    def second_application(b):
        hand_on_first(b)
        inner_terms(ext2, b, 1)
        hand_on_last(b)
        wait_halos(b, 1, False)
        target = jnp.where(paired & (b < 2), norb + 2 * core + b, b)

        def store(x, first, place, total):
            before = ext1[b, pl.ds(pl.multiple_of(reach_rows + x * ny + first, 8), 8), :]
            fields[target, place, :] = 2.0 * total - before

        along_x(ext2, b, store)
        root_sends(b)
        hand_on_next(b)

        @pl.when(paired & (b == 1))
        def _():
            @pl.when(core == 1)
            def _():
                @pl.loop(0, norb)
                def _(o):
                    send_halos(o, 0)

            @pl.loop(2, norb)
            def _(late):
                first_coefficients(late)

    @pl.loop(0, 2 * norb)
    def _(i):
        first = jnp.where(paired, i % 4 < 2, i < norb)
        b = jnp.where(paired, i // 4 * 2 + i % 2, i % norb)

        @pl.when(first)
        def _():
            first_application(b)

        @pl.when(jnp.logical_not(first))
        def _():
            second_application(b)

    for b in range(norb):
        given = (core == 1) & jnp.logical_not(paired) | paired & (core != b // 2)

        @pl.when(given)
        def _():
            sibling_copy(b).wait_recv()

    @pl.when(band == 1)
    def _():
        for b in range(2):
            back_copy(b).wait_recv()

    couples = [(k, m) for k in range(norb) for m in range(k + 1)]
    n_pairs = len(couples) + norb * norb

    def add_pairs(t, sums):
        place = pl.ds(pl.multiple_of(t * 8, 8), 8)
        p = [panel[k, place, :] for k in range(norb)]
        f = [filt[n, place, :] for n in range(norb)]
        terms = [p[k] * p[m] for k, m in couples] + [p[k] * f[n] for k in range(norb) for n in range(norb)]
        return tuple(s + term for s, term in zip(sums, terms))

    sums = lax.fori_loop(
        0, plane_rows // 8, add_pairs, tuple(jnp.zeros((8, LANES), f32) for _ in range(n_pairs))
    )
    pairs[...] = jnp.zeros(pairs.shape, f32)
    for i, s in enumerate(sums):
        pairs[i : i + 1, :] = jnp.sum(s, axis=0, keepdims=True)
    gram_out[...] = jnp.sum(pairs[...].T.reshape(LANES // 8, 8, LANES), axis=0)

    def gram_copy(step):
        return pltpu.make_async_remote_copy(
            src_ref=gram_out, dst_ref=gram_in.at[step],
            send_sem=gram_send.at[step], recv_sem=gram_recv.at[step],
            device_id=(band, peer(step)), device_id_type=MESH,
        )

    for step in range(1, n_grid):
        gram_copy(step).start()
    total = gram_out[...]
    for step in range(1, n_grid):
        gram_copy(step).wait_recv()
        total = total + gram_in[step]
    total = jnp.sum(total, axis=0, keepdims=True) * (1.0 / (plane_rows * LANES * n_grid))
    lane1 = lax.broadcasted_iota(jnp.int32, (1, LANES), 1)

    def number(i):
        one = jnp.sum(jnp.where(lane1 == i, total, 0.0), axis=1, keepdims=True)
        return jnp.broadcast_to(one, (8, LANES))

    gram = {couple: number(i) for i, couple in enumerate(couples)}
    raw = [[number(len(couples) + k * norb + n) for n in range(norb)] for k in range(norb)]
    lower, inverse = {}, {}
    for j in range(norb):
        left = gram[j, j]
        for m in range(j):
            left = left - lower[j, m] * lower[j, m]
        lower[j, j] = jnp.sqrt(left)
        inverse[j, j] = 1.0 / lower[j, j]
        for i in range(j + 1, norb):
            left = gram[i, j]
            for m in range(j):
                left = left - lower[i, m] * lower[j, m]
            lower[i, j] = left * inverse[j, j]
    for j in range(norb):
        for i in range(j + 1, norb):
            left = lower[i, j] * inverse[j, j]
            for m in range(j + 1, i):
                left = left + lower[i, m] * inverse[m, j]
            inverse[i, j] = -left * inverse[i, i]
    corr = [
        [sum(inverse[k, m] * raw[m][n] for m in range(k + 1)) for n in range(norb)]
        for k in range(norb)
    ]
    weight = [[None] * norb for _ in range(norb)]
    zero8 = jnp.zeros((8, LANES), f32)
    for m in range(norb):
        for n in range(norb):
            away = -sum(inverse[k, m] * corr[k][n] for k in range(m, norb))
            weight[m][n] = jnp.where(root, inverse[n, m] if m <= n else zero8, away)
    keep = jnp.where(root, zero8, jnp.ones((8, LANES), f32))

    @pl.loop(0, plane_rows // 8)
    def _(t):
        place = pl.ds(pl.multiple_of(t * 8, 8), 8)
        p = [panel[k, place, :] for k in range(norb)]
        for n in range(norb):
            value = keep * filt[n, place, :]
            for m in range(norb):
                value = value + weight[m][n] * p[m]
            out_ref[n, place, :] = value

    @pl.loop(0, norb)
    def _(b):
        wait_halos(b, 0, True)
        wait_halos(b, 1, True)
        for app in range(2):
            for d in range(len(COEF_STEPS)):
                coef_copy(app, b, d).wait_send()

        def ended(copy):
            copy.wait_send()

        @pl.when(paired & (core == b // 2))
        def _():
            for y in range(1, n_y):
                scatter_copy(b, y).wait_send()
            z_copies(b, ended)
            y_copies(b, ended)
            sibling_copy(b).wait_send()

        @pl.when(follower)
        def _():
            @pl.when(zh == 0)
            def _():
                z_copies(b, ended)

            if ringed:
                for z, way in ((1, 0), (3, 1)):
                    @pl.when(zh == z)
                    def _():
                        z_copy(b, way).wait_send()

            y_copies(b, ended)
            sibling_copy(b).wait_send()

        @pl.when(jnp.logical_not(stays(b)))
        def _():
            swap_copy(b).wait_send()

        @pl.when(root & (b < 2))
        def _():
            back_copy(b).wait_send()

    for k in range(2):
        coup_copy(k).wait_send()
    for step in range(1, n_grid):
        gram_copy(step).wait_send()


def local(n_band, n_grid, orbitals, potential, projectors, coupling, entry_cell, entry_atom):
    norb, nx, ny, nz = orbitals.shape
    ent = entry_cell.shape[0]
    rows = nx * ny
    chips = n_band // 2
    f32, bf16 = jnp.float32, jnp.bfloat16
    vmem, dma = pltpu.VMEM, pltpu.SemaphoreType.DMA
    ext_rows = rows + 2 * REACH * ny
    whole = pl.BlockSpec(memory_space=pltpu.VMEM)
    out = pl.pallas_call(
        functools.partial(kernel, n_band, n_grid, nx, ny, ent),
        out_shape=jax.ShapeDtypeStruct((norb, rows, nz), f32),
        in_specs=[pl.BlockSpec(memory_space=pltpu.HBM)] * 6,
        out_specs=whole,
        scratch_shapes=[
            vmem((rows, nz), f32),
            vmem(projectors.shape, f32),
            vmem((4, 4, ATOM_DEV), f32),
            vmem((1, ent), jnp.int32),
            vmem((1, ent), jnp.int32),
            vmem((norb, ext_rows, nz), f32),
            vmem((norb, ext_rows, nz), f32),
            vmem((2 * norb, rows, nz), f32),
            vmem((ent, rows), bf16),
            vmem((rows, ent), bf16),
            vmem((ent, LANES), bf16),
            vmem((2 * LANES, ent), bf16),
            vmem((ent, 2 * LANES), bf16),
            vmem((ent, 2 * LANES), bf16),
            vmem((ent, 2 * LANES), bf16),
            vmem((norb, rows, 2 * LANES), bf16),
            vmem((norb, rows, LANES), f32),
            vmem((2 * LANES, 2 * LANES), bf16),
            vmem((2 * LANES, 2 * LANES), bf16),
            vmem((ent, 8), f32),
            vmem((2, norb, 8, LANES), f32),
            vmem((2, norb, 4, 8, LANES), f32),
            vmem((8, LANES), f32),
            vmem((2, 8, LANES), f32),
            vmem((32, LANES), f32),
            vmem((LANES, LANES), f32),
            vmem((8, LANES), f32),
            vmem((n_grid, 8, LANES), f32),
            dma((5,)),
            dma((norb,)),
            dma((norb,)), dma((2,)), dma((2,)),
            dma((2, norb, 2)), dma((2, norb, 2)),
            dma((2, norb, 4)), dma((2, norb, 4)),
            dma((2,)), dma((2,)),
            dma((norb, 4)), dma((norb,)),
            dma((norb, 2)), dma((norb, 2)),
            dma((norb, 2)), dma((norb, 2)),
            dma((norb, 4)), dma((norb,)),
            dma((norb,)), dma((norb,)),
            dma((n_grid,)), dma((n_grid,)),
        ],
        compiler_params=pltpu.CompilerParams(
            collective_id=0, has_side_effects=True, vmem_limit_bytes=40 * 1024 * 1024
        ),
        name="filter_panel",
    )(
        *[pltpu.with_memory_space_constraint(v, pltpu.HBM) for v in (orbitals.reshape(norb, rows, nz),
        potential.reshape(rows, nz),
        projectors,
        coupling.transpose(1, 2, 0),
        entry_cell.reshape(1, ent),
        entry_atom.reshape(1, ent))]
    )
    return out.reshape(orbitals.shape)


def solution(mesh):
    return jax.shard_map(
        functools.partial(local, mesh.shape["band"], mesh.shape["grid"]),
        mesh=mesh,
        in_specs=(
            P("band", "grid", None, None),
            P("grid", None, None),
            P(None, "grid"),
            P("grid", None, None),
            P("grid"),
            P("grid"),
        ),
        out_specs=P("band", "grid", None, None),
        check_vma=False,
    )
```
